256 devices in a mesh: dp: 8 (over x, y_hi), dap: 32 (over y_lo, z, core).
Axes of the slice: x: 4, y: 4 (y_hi: 2, y_lo: 2; y = y_hi * 2 + y_lo), z: 8, core: 2. Of those that a mesh axis runs over, the one named last changes fastest.
Arguments:
- pair: bfloat16 [2048, 256, 128], P(('dp', 'dap')), parts along dimension 0, may hold values from -6 to 6
- gain_in: float32 [128], replicated, may hold values from 0.1 to 1.9
- w_proj: bfloat16 [128, 640], replicated, may hold values from -0.5 to 0.5
- gain_out: float32 [128], replicated, may hold values from 0.1 to 1.9
- w_out: bfloat16 [128, 128], replicated, may hold values from -0.5 to 0.5
- cotangent: bfloat16 [2048, 256, 128], P(('dp', 'dap')), parts along dimension 0, may hold values from -6 to 6
Outputs:
- update: bfloat16 [2048, 256, 128], P(('dp', 'dap')), parts along dimension 0
- grad_pair: bfloat16 [2048, 256, 128], P(('dp', 'dap')), parts along dimension 0
- grad_gain_in: float32 [1024], P('dp'), parts along dimension 0
- grad_w_proj: float32 [1024, 640], P('dp'), parts along dimension 0
- grad_gain_out: float32 [1024], P('dp'), parts along dimension 0
- grad_w_out: float32 [1024, 128], P('dp'), parts along dimension 0
The draws below stay inside these ranges and needn't reach their ends.
There are 8 independent parts, one for each index of `dp`. The reference program is written for one: setup_inputs(seed, part) draws one part's arguments, and reference() takes and returns one part's arrays. A program takes and returns all parts, laid end to end along the dimension named above; an argument that names none is the same for every part. Nothing has to cross between parts.
All inputs are finite; a program needn't handle non-finite values.
Results may differ from the reference program's by a relative error of at most 0.035.
Values may be sent and summed in bfloat16 or wider, within the bound.
No kernel may reach another device: no remote copies, remote signals or barrier semaphores. Data moves between devices by JAX's collectives and lax.ppermute only.
A program may use at most 320 MiB of HBM per device.

```python
import jax
import jax.numpy as jnp
from jax import lax

CH = 128
HID = 128
NRES = 256


def levels(stream_key, extent, cuts, low, high):
    def one(position, parts):
        draws = jax.random.uniform(jax.random.fold_in(jax.random.fold_in(stream_key, 6), position), (parts,), jnp.float32, low / len(cuts), high / len(cuts))
        return jnp.repeat(jnp.exp(draws), extent[position] // parts).reshape((-1,) + (1,) * (len(extent) - position - 1))

    factor_of = one(*cuts[0])
    for cut in cuts[1:]:
        factor_of = factor_of * one(*cut)
    return factor_of


def bell_draw(rng, shape, spread, reach, pieces=(), dtype=jnp.bfloat16):
    entries = jax.random.normal(rng, shape, jnp.float32) * spread
    if len(pieces) > 0:
        entries = levels(rng, shape, pieces, -0.22, 0.18) * entries
    return jnp.clip(entries, min=-reach, max=reach).astype(dtype)


def setup_inputs(seed: int = 0, part: int = 0) -> dict:
    keys = jax.random.split(jax.random.key(seed), 7)
    part_splits = jax.random.split(jax.random.fold_in(keys[6], part), 7)
    pair = bell_draw(part_splits[0], (NRES, NRES, CH), 1.0, 6.0, ((0, 32),))
    gain_in = jnp.clip(1.0 + 0.18 * jax.random.normal(keys[1], (CH,), jnp.float32), 0.1, 1.9)
    w_proj = bell_draw(keys[2], (CH, 4 * HID + CH), CH ** -0.5, 0.5)
    gain_out = jnp.clip(1.0 + 0.18 * jax.random.normal(keys[3], (HID,), jnp.float32), 0.1, 1.9)
    w_out = bell_draw(keys[4], (HID, CH), HID ** -0.5, 0.5)
    cotangent = bell_draw(part_splits[5], (NRES, NRES, CH), 1.0, 6.0, ((0, 32),))
    return dict(pair=pair, gain_in=gain_in, w_proj=w_proj, gain_out=gain_out, w_out=w_out, cotangent=cotangent)


def channel_norm(values):
    mean_val = lax.optimization_barrier(jnp.mean(values, axis=-1, keepdims=True))
    shifted = values - mean_val
    variance = lax.optimization_barrier(jnp.mean(shifted * shifted, axis=-1, keepdims=True))
    inv_std = lax.rsqrt(variance + 1e-05)
    return (shifted * inv_std, inv_std)

def norm_grad(scaled, centred, inv_std):
    first = lax.optimization_barrier(jnp.mean(scaled, axis=-1, keepdims=True))
    second = lax.optimization_barrier(jnp.mean(scaled * centred, axis=-1, keepdims=True))
    return inv_std * (scaled - first - centred * second)

def reference(pair, gain_in, w_proj, gain_out, w_out, cotangent):
    width = gain_out.shape[0]
    centred, inv_std = channel_norm(pair.astype(jnp.float32))
    normed = (centred * gain_in).astype(jnp.bfloat16)
    projected = jnp.dot(normed, w_proj, preferred_element_type=jnp.float32)
    left_val = projected[..., 0:width]
    left_sig = jax.nn.sigmoid(projected[..., width:2 * width])
    right_val = projected[..., 2 * width:3 * width]
    right_sig = jax.nn.sigmoid(projected[..., 3 * width:4 * width])
    out_gate = jax.nn.sigmoid(projected[..., 4 * width:])
    left_edge = (left_sig * left_val).astype(jnp.bfloat16)
    right_edge = (right_sig * right_val).astype(jnp.bfloat16)
    triangle = jnp.einsum('ikc,jkc->ijc', left_edge.astype(jnp.float32), right_edge.astype(jnp.float32))
    tri_centred, tri_inv_std = channel_norm(triangle)
    out_normed = (tri_centred * gain_out).astype(jnp.bfloat16)
    out_proj = jnp.dot(out_normed, w_out, preferred_element_type=jnp.float32)
    update = (out_gate * out_proj).astype(jnp.bfloat16)
    grad_upd = cotangent.astype(jnp.float32)
    grad_gate = grad_upd * out_proj
    grad_proj_out = (grad_upd * out_gate).astype(jnp.bfloat16)
    grad_w_out = jnp.einsum('ijh,ijc->hc', out_normed.astype(jnp.float32), grad_proj_out.astype(jnp.float32))
    grad_normed_out = jnp.dot(grad_proj_out, w_out.T, preferred_element_type=jnp.float32)
    grad_gain_out = lax.optimization_barrier(jnp.sum(grad_normed_out * tri_centred, axis=(0, 1)))
    grad_triangle = norm_grad(grad_normed_out * gain_out, tri_centred, tri_inv_std).astype(jnp.bfloat16)
    grad_left = jnp.einsum('ijc,jkc->ikc', grad_triangle.astype(jnp.float32), right_edge.astype(jnp.float32))
    grad_right = jnp.einsum('ijc,ikc->jkc', grad_triangle.astype(jnp.float32), left_edge.astype(jnp.float32))
    grad_projected = jnp.concatenate([grad_left * left_sig, grad_left * left_val * left_sig * (1.0 - left_sig), grad_right * right_sig, grad_right * right_val * right_sig * (1.0 - right_sig), grad_gate * out_gate * (1.0 - out_gate)], axis=-1).astype(jnp.bfloat16)
    grad_w_proj = jnp.einsum('ijc,ijd->cd', normed.astype(jnp.float32), grad_projected.astype(jnp.float32))
    grad_normed = jnp.dot(grad_projected, w_proj.T, preferred_element_type=jnp.float32)
    grad_gain_in = lax.optimization_barrier(jnp.sum(grad_normed * centred, axis=(0, 1)))
    grad_pair = norm_grad(grad_normed * gain_in, centred, inv_std).astype(jnp.bfloat16)
    return (update, grad_pair, grad_gain_in, grad_w_proj, grad_gain_out, grad_w_out)
```

```python
import jax
import jax.numpy as jnp
from jax import lax
from jax.sharding import PartitionSpec as P


def channel_norm(values):
    mean_val = jnp.mean(values, axis=-1, keepdims=True)
    shifted = values - mean_val
    variance = jnp.mean(shifted * shifted, axis=-1, keepdims=True)
    inv_std = lax.rsqrt(variance + 1e-05)
    return (shifted * inv_std, inv_std)


def norm_grad(scaled, centred, inv_std):
    first = jnp.mean(scaled, axis=-1, keepdims=True)
    second = jnp.mean(scaled * centred, axis=-1, keepdims=True)
    return inv_std * (scaled - first - centred * second)


def exchange(values):
    return lax.all_to_all(values, "dap", 0, 0, tiled=True)


def local(devices, pair, gain_in, w_proj, gain_out, w_out, cotangent):
    width = gain_out.shape[0]
    rows, res, _ = pair.shape
    share = width // devices
    f32, bf16 = jnp.float32, jnp.bfloat16

    def to_channels(values):
        sent = jnp.stack([v.astype(bf16) for v in values])
        sent = sent.reshape(len(values), rows, res, devices, share).transpose(3, 0, 4, 1, 2)
        got = exchange(sent)
        return got.transpose(1, 2, 0, 3, 4).reshape(len(values), share, devices * rows, res)

    def to_rows(values):
        sent = values.astype(bf16).reshape(-1, share, devices, rows, res).transpose(2, 0, 1, 3, 4)
        got = exchange(sent)
        return got.transpose(1, 3, 4, 0, 2).reshape(-1, rows, res, width)

    centred, inv_std = channel_norm(pair.astype(f32))
    normed = (centred * gain_in).astype(bf16)
    projected = jnp.dot(normed, w_proj, preferred_element_type=f32)
    left_val = projected[..., 0:width]
    left_sig = jax.nn.sigmoid(projected[..., width : 2 * width])
    right_val = projected[..., 2 * width : 3 * width]
    right_sig = jax.nn.sigmoid(projected[..., 3 * width : 4 * width])
    out_gate = jax.nn.sigmoid(projected[..., 4 * width :])
    edges = to_channels([left_sig * left_val, right_sig * right_val])
    left, right = edges[0], edges[1]
    triangle = jnp.einsum("cik,cjk->cij", left, right, preferred_element_type=f32)
    triangle = to_rows(triangle)[0].astype(f32)
    tri_centred, tri_inv_std = channel_norm(triangle)
    out_normed = (tri_centred * gain_out).astype(bf16)
    out_proj = jnp.dot(out_normed, w_out, preferred_element_type=f32)
    update = (out_gate * out_proj).astype(bf16)
    grad_upd = cotangent.astype(f32)
    grad_gate = grad_upd * out_proj
    grad_proj_out = (grad_upd * out_gate).astype(bf16)
    grad_w_out = jnp.einsum("ijh,ijc->hc", out_normed, grad_proj_out, preferred_element_type=f32)
    grad_normed_out = jnp.einsum("ijc,hc->ijh", grad_proj_out, w_out, preferred_element_type=f32)
    grad_gain_out = jnp.sum(grad_normed_out * tri_centred, axis=(0, 1))
    grad_triangle = norm_grad(grad_normed_out * gain_out, tri_centred, tri_inv_std)
    grad_tri = to_channels([grad_triangle])[0]
    grad_left = jnp.einsum("cij,cjk->cik", grad_tri, right, preferred_element_type=f32)
    grad_right = jnp.einsum("cij,cik->cjk", grad_tri, left, preferred_element_type=f32)
    grads = to_rows(jnp.stack([grad_left, grad_right])).astype(f32)
    grad_left, grad_right = grads[0], grads[1]
    grad_projected = jnp.concatenate(
        [
            grad_left * left_sig,
            grad_left * left_val * left_sig * (1.0 - left_sig),
            grad_right * right_sig,
            grad_right * right_val * right_sig * (1.0 - right_sig),
            grad_gate * out_gate * (1.0 - out_gate),
        ],
        axis=-1,
    ).astype(bf16)
    grad_w_proj = jnp.einsum("ijc,ijd->cd", normed, grad_projected, preferred_element_type=f32)
    grad_normed = jnp.einsum("ijd,cd->ijc", grad_projected, w_proj, preferred_element_type=f32)
    grad_gain_in = jnp.sum(grad_normed * centred, axis=(0, 1))
    grad_pair = norm_grad(grad_normed * gain_in, centred, inv_std).astype(bf16)

    blocks = [grad_w_proj[:, b * width : (b + 1) * width] for b in range(5)] + [grad_w_out]
    matrices = jnp.concatenate(blocks, axis=0).astype(bf16).reshape(devices, -1, width)
    gains = jnp.stack([grad_gain_in, grad_gain_out]).astype(bf16)
    gains = jnp.broadcast_to(gains[None], (devices, 2, width))
    got = exchange(jnp.concatenate([matrices, gains], axis=1)).astype(f32)
    total = jnp.sum(got, axis=0)
    gains = total[-2:]
    mine = total[:-2].astype(bf16)
    full = exchange(jnp.broadcast_to(mine[None], (devices,) + mine.shape))
    full = full.astype(f32).reshape(6, width, width)
    grad_w_proj = jnp.concatenate([full[b] for b in range(5)], axis=1)
    return (update, grad_pair, gains[0], grad_w_proj, gains[1], full[5])


def solution(mesh):
    devices = mesh.shape["dap"]

    def program(*args):
        return local(devices, *args)

    in_specs = (P(("dp", "dap"), None, None), P(), P(), P(), P(), P(("dp", "dap"), None, None))
    out_specs = (
        P(("dp", "dap"), None, None),
        P(("dp", "dap"), None, None),
        P("dp"),
        P("dp", None),
        P("dp"),
        P("dp", None),
    )
    return jax.shard_map(program, mesh=mesh, in_specs=in_specs, out_specs=out_specs, check_vma=False)
```

```python
import functools

import jax
import jax.numpy as jnp
from jax import lax
from jax.experimental import pallas as pl
from jax.experimental.pallas import tpu as pltpu
from jax.sharding import PartitionSpec as P

F32, BF16 = jnp.float32, jnp.bfloat16
EPS = 1e-05
LANES = 128


def exchange(values):
    return lax.all_to_all(values, "dap", 0, 0, tiled=True)


def hold(*values):
    return lax.optimization_barrier(values)


def call(kernel, out_shape, operands, scratch=(), flops=0):
    leaves = out_shape if isinstance(out_shape, (tuple, list)) else [out_shape]
    moved = sum(a.size * a.dtype.itemsize for a in list(operands) + list(leaves))
    spec = pl.BlockSpec(memory_space=pltpu.VMEM)
    out_specs = [spec] * len(out_shape) if isinstance(out_shape, (tuple, list)) else spec
    return pl.pallas_call(
        kernel,
        out_shape=out_shape,
        in_specs=[spec] * len(operands),
        out_specs=out_specs,
        scratch_shapes=list(scratch),
        cost_estimate=pl.CostEstimate(flops=flops, bytes_accessed=moved, transcendentals=0),
        compiler_params=pltpu.CompilerParams(vmem_limit_bytes=48 * 1024 * 1024),
    )(*operands)


def norm_rows(values):
    width = values.shape[0]
    shifted = values - jnp.sum(values, axis=0, keepdims=True) * (1.0 / width)
    variance = jnp.sum(shifted * shifted, axis=0, keepdims=True) * (1.0 / width)
    inv_std = lax.rsqrt(variance + EPS)
    return shifted * inv_std, inv_std


def put_row(ref, i, rows, values):
    for h in range(ref.shape[0]):
        spots = pl.ds(i, values.shape[0], stride=rows)
        ref[h, spots, :] = values[:, h * LANES : (h + 1) * LANES]


def take_row(ref, i, rows):
    spots = pl.ds(i, ref.shape[1] // rows, stride=rows)
    return jnp.concatenate([ref[h, spots, :] for h in range(ref.shape[0])], axis=1)


def fill(got_ref, left_ref, right_ref):
    devices, both, _ = got_ref.shape
    half = both // 2
    for n, ref in enumerate((left_ref, right_ref)):
        for h in range(ref.shape[0]):
            block = got_ref[:, n * half : (n + 1) * half, h * LANES : (h + 1) * LANES]
            ref[h] = block.astype(F32).reshape(devices * half, LANES)


def edges_kernel(pair_ref, gain_ref, weight_ref, sent_ref, left_ref, right_ref):
    rows, res, width = pair_ref.shape
    devices = sent_ref.shape[0]
    half = sent_ref.shape[1] // 2
    weight = weight_ref[...].astype(F32).T.astype(BF16)
    gain = gain_ref[...]
    for i in range(rows):
        centred, _ = norm_rows(pair_ref[i].astype(F32).T)
        normed = (centred * gain).astype(BF16)
        out = jnp.dot(weight, normed, preferred_element_type=F32)
        put_row(left_ref, i, rows, jax.nn.sigmoid(out[width : 2 * width]) * out[:width])
        put_row(right_ref, i, rows, jax.nn.sigmoid(out[3 * width :]) * out[2 * width : 3 * width])
    for n, ref in enumerate((left_ref, right_ref)):
        for h in range(res // LANES):
            block = ref[h].reshape(devices, half, LANES).astype(BF16)
            sent_ref[:, n * half : (n + 1) * half, h * LANES : (h + 1) * LANES] = block


def matrices_of(ref, first, share, rows):
    devices, _, res = ref.shape
    block = ref[:, first : first + share * rows, :].astype(F32)
    block = block.reshape(devices, share, rows, res)
    return [block[:, c].reshape(devices * rows, res).astype(BF16) for c in range(share)]


def store_matrices(ref, first, values, rows):
    devices, _, res = ref.shape
    block = jnp.stack([v.reshape(devices, rows, res) for v in values], axis=1)
    ref[:, first : first + len(values) * rows, :] = block.reshape(
        devices, len(values) * rows, res
    ).astype(BF16)


NT = (((1,), (1,)), ((), ()))


def triangle_kernel(share, rows, got_ref, sent_ref):
    half = share * rows
    left = matrices_of(got_ref, 0, share, rows)
    right = matrices_of(got_ref, half, share, rows)
    out = [lax.dot_general(a, b, NT, preferred_element_type=F32) for a, b in zip(left, right)]
    store_matrices(sent_ref, 0, out, rows)


def norm_grad_kernel(rows, got_ref, scaled_ref, sent_ref):
    devices, block, res = got_ref.shape
    share = block // rows
    width = devices * share

    def over_share(values):
        return jnp.sum(values.reshape(share, rows, res), axis=0)

    zero = jnp.zeros((rows, res), F32)

    def add_up(d, carry):
        return carry + over_share(got_ref[d].astype(F32))

    mean = lax.fori_loop(0, devices, add_up, zero, unroll=4) * (1.0 / width)
    mean = jnp.concatenate([mean] * share, axis=0)

    def second(d, carry):
        shifted = got_ref[d].astype(F32) - mean
        return (
            carry[0] + over_share(shifted * shifted),
            carry[1] + over_share(shifted * scaled_ref[d]),
        )

    variance, product = lax.fori_loop(0, devices, second, (zero, zero), unroll=4)
    inv_std = lax.rsqrt(variance * (1.0 / width) + EPS)
    product = product * (1.0 / width) * inv_std * inv_std * inv_std
    inv_std = jnp.concatenate([inv_std] * share, axis=0)
    product = jnp.concatenate([product] * share, axis=0)

    def write(d, carry):
        shifted = got_ref[d].astype(F32) - mean
        sent_ref[d] = (inv_std * scaled_ref[d] - shifted * product).astype(BF16)
        return carry

    lax.fori_loop(0, devices, write, 0, unroll=4)


def edge_grads_kernel(share, rows, got_ref, left_ref, right_ref, sent_ref):
    grads = matrices_of(got_ref, 0, share, rows)
    left_grads, right_grads = [], []
    for c in range(share):
        left_grads.append(jnp.dot(grads[c], right_ref[c], preferred_element_type=F32))
        turned = grads[c].astype(F32).T.astype(BF16)
        right_grads.append(jnp.dot(turned, left_ref[c], preferred_element_type=F32))
    store_matrices(sent_ref, 0, left_grads, rows)
    store_matrices(sent_ref, share * rows, right_grads, rows)


def weight_grads_kernel(got_ref, factor_ref, normed_ref, early_ref, sent_ref, left_ref, right_ref):
    rows, width, _ = normed_ref.shape
    fill(got_ref, left_ref, right_ref)
    total = None
    for i in range(rows):
        left, right = take_row(left_ref, i, rows), take_row(right_ref, i, rows)
        factor = factor_ref[i]
        normed = normed_ref[i]
        parts = []
        for b, grad in enumerate((left, left, right, right)):
            grad = (grad * factor[b * width : (b + 1) * width]).astype(BF16)
            parts.append(lax.dot_general(normed, grad, NT, preferred_element_type=F32))
        total = parts if total is None else [a + b for a, b in zip(total, parts)]
    blocks = jnp.concatenate(total + [early_ref[...]], axis=0)
    sent_ref[...] = blocks.reshape(sent_ref.shape).astype(BF16)


def pair_grad_kernel(
    got_ref, factor_ref, gate_ref, pair_ref, gain_ref, weight_ref, out_ref, left_ref, right_ref
):
    rows, _, width = pair_ref.shape
    fill(got_ref, left_ref, right_ref)
    weight = weight_ref[...]
    gain = gain_ref[...]
    for i in range(rows):
        left, right = take_row(left_ref, i, rows), take_row(right_ref, i, rows)
        factor = factor_ref[i]
        parts = [
            (grad * factor[b * width : (b + 1) * width]).astype(BF16)
            for b, grad in enumerate((left, left, right, right))
        ]
        grads = jnp.concatenate(parts + [gate_ref[i]], axis=0)
        scaled = jnp.dot(weight, grads, preferred_element_type=F32) * gain
        centred, inv_std = norm_rows(pair_ref[i].astype(F32).T)
        first = jnp.sum(scaled, axis=0, keepdims=True) * (1.0 / width)
        second = jnp.sum(scaled * centred, axis=0, keepdims=True) * (1.0 / width)
        grad_pair = inv_std * (scaled - first - centred * second)
        out_ref[i] = grad_pair.T.astype(BF16)


def finish_kernel(full_ref, weight_ref, w_out_ref, gain_in_ref, gain_out_ref, *outs):
    grad_weight_ref, grad_out_ref, grad_gain_in_ref, grad_gain_out_ref = outs
    width = w_out_ref.shape[0]
    full = full_ref[...].astype(F32).reshape(6 * width, width)
    weight = weight_ref[...].astype(F32)
    total = jnp.zeros((width, width), F32)
    for b in range(5):
        block = full[b * width : (b + 1) * width]
        grad_weight_ref[:, b * width : (b + 1) * width] = block
        total = total + block * weight[:, b * width : (b + 1) * width]
    block = full[5 * width :]
    grad_out_ref[...] = block
    total_out = block * w_out_ref[...].astype(F32)
    grad_gain_in_ref[...] = jnp.sum(total.T, axis=0, keepdims=True) / gain_in_ref[...]
    grad_gain_out_ref[...] = jnp.sum(total_out.T, axis=0, keepdims=True) / gain_out_ref[...]


def local(devices, pair, gain_in, w_proj, gain_out, w_out, cotangent):
    width = gain_out.shape[0]
    rows, res, _ = pair.shape
    share = width // devices
    half = share * rows
    shape = jax.ShapeDtypeStruct
    scratch = [pltpu.VMEM((res // LANES, width * rows, LANES), F32)] * 2

    def mean_c(values):
        return jnp.mean(values, axis=1, keepdims=True)

    def channel_norm(values):
        shifted = values - mean_c(values)
        inv_std = lax.rsqrt(mean_c(shifted * shifted) + EPS)
        return shifted * inv_std, inv_std

    gain_in_col, gain_out_col = gain_in[:, None], gain_out[:, None]
    sent = call(
        edges_kernel,
        shape((devices, 2 * half, res), BF16),
        (pair, gain_in_col, w_proj[:, : 4 * width]),
        scratch,
    )
    sent, pair, cotangent = hold(sent, pair, cotangent)
    got = exchange(sent)

    centred, _ = channel_norm(pair.transpose(0, 2, 1).astype(F32))
    normed = (centred * gain_in_col[None]).astype(BF16)
    projected = jnp.einsum("cd,ick->idk", w_proj, normed, preferred_element_type=F32)
    left_val, left_gate, right_val, right_gate, out_gate = [
        projected[:, b * width : (b + 1) * width] for b in range(5)
    ]
    left_sig, right_sig = jax.nn.sigmoid(left_gate), jax.nn.sigmoid(right_gate)
    factor = jnp.concatenate(
        [
            left_sig,
            left_val * left_sig * (1.0 - left_sig),
            right_sig,
            right_val * right_sig * (1.0 - right_sig),
        ],
        axis=1,
    )
    out_gate = jax.nn.sigmoid(out_gate)
    cot = cotangent.transpose(0, 2, 1).astype(F32)
    grad_proj_out = (cot * out_gate).astype(BF16)
    scaled = jnp.einsum("hc,ick->ihk", w_out, grad_proj_out, preferred_element_type=F32)
    scaled = scaled * gain_out_col[None]
    scaled = scaled - mean_c(scaled)
    scaled = scaled.transpose(1, 0, 2).reshape(devices, half, res)

    got, normed, factor, out_gate, cot, grad_proj_out, scaled = hold(
        got, normed, factor, out_gate, cot, grad_proj_out, scaled
    )
    sent = call(
        functools.partial(triangle_kernel, share, rows), shape((devices, half, res), BF16), (got,)
    )
    sent, got = hold(sent, got)
    edges = got.reshape(devices, 2, share, rows, res).transpose(1, 2, 0, 3, 4)
    edges = edges.reshape(2, share, devices * rows, res)
    got = exchange(sent)
    got, edges = hold(got, edges)
    sent = call(
        functools.partial(norm_grad_kernel, rows),
        shape((devices, half, res), BF16),
        (got, scaled),
    )
    sent, triangle = hold(sent, got)
    got = exchange(sent)

    triangle = triangle.reshape(width, rows, res).transpose(1, 0, 2).astype(F32)
    tri_centred, _ = channel_norm(triangle)
    out_normed = (tri_centred * gain_out_col[None]).astype(BF16)
    out_proj = jnp.einsum("hc,ihk->ick", w_out, out_normed, preferred_element_type=F32)
    update = (out_gate * out_proj).astype(BF16).transpose(0, 2, 1)
    grad_gate = (cot * out_proj * out_gate * (1.0 - out_gate)).astype(BF16)
    grad_w_gate = jnp.einsum("ick,idk->cd", normed, grad_gate, preferred_element_type=F32)
    grad_w_out = jnp.einsum("ihk,ick->hc", out_normed, grad_proj_out, preferred_element_type=F32)
    early = jnp.concatenate([grad_w_gate, grad_w_out], axis=0)
    got, early, grad_gate, update = hold(got, early, grad_gate, update)

    sent = call(
        functools.partial(edge_grads_kernel, share, rows),
        shape((devices, 2 * half, res), BF16),
        (got, edges[0], edges[1]),
    )
    got = exchange(sent)
    sent = call(
        weight_grads_kernel,
        shape((devices, 6 * width // devices, width), BF16),
        (got, factor, normed, early),
        scratch,
    )
    sent, edge_grads, factor = hold(sent, got, factor)
    got = exchange(sent)
    grad_pair = call(
        pair_grad_kernel,
        shape((rows, res, width), BF16),
        (edge_grads, factor, grad_gate, pair, gain_in_col, w_proj),
        scratch,
        flops=2 * rows * res * width * 5 * width,
    )
    mine = jnp.sum(got.astype(F32), axis=0).astype(BF16)
    full = exchange(jnp.broadcast_to(mine[None], (devices,) + mine.shape))
    grad_w_proj, grad_w_out, grad_gain_in, grad_gain_out = call(
        finish_kernel,
        (
            shape((width, 5 * width), F32),
            shape((width, width), F32),
            shape((1, width), F32),
            shape((1, width), F32),
        ),
        (full, w_proj, w_out, gain_in[None], gain_out[None]),
    )
    return (update, grad_pair, grad_gain_in[0], grad_w_proj, grad_gain_out[0], grad_w_out)


def solution(mesh):
    devices = mesh.shape["dap"]

    def program(*args):
        return local(devices, *args)

    in_specs = (P(("dp", "dap"), None, None), P(), P(), P(), P(), P(("dp", "dap"), None, None))
    out_specs = (
        P(("dp", "dap"), None, None),
        P(("dp", "dap"), None, None),
        P("dp"),
        P("dp", None),
        P("dp"),
        P("dp", None),
    )
    return jax.shard_map(program, mesh=mesh, in_specs=in_specs, out_specs=out_specs, check_vma=False)
```

```python
import functools

import jax
import jax.numpy as jnp
from jax import lax
from jax.experimental import pallas as pl
from jax.experimental.pallas import tpu as pltpu
from jax.sharding import PartitionSpec as P

F32, BF16 = jnp.float32, jnp.bfloat16
EPS = 1e-05
LANES = 128
NT = (((1,), (1,)), ((), ()))


def exchange(values):
    return lax.all_to_all(values, "dap", 0, 0, tiled=True)


def hold(*values):
    return lax.optimization_barrier(values)


def call(kernel, out_shape, operands, scratch=(), flops=0, outside=0, limit=16):
    leaves = out_shape if isinstance(out_shape, (tuple, list)) else [out_shape]
    moved = sum(a.size * a.dtype.itemsize for a in list(operands) + list(leaves))
    spec = pl.BlockSpec(memory_space=pltpu.VMEM)
    out_specs = [spec] * len(out_shape) if isinstance(out_shape, (tuple, list)) else spec
    return pl.pallas_call(
        kernel,
        out_shape=out_shape,
        in_specs=[pl.BlockSpec(memory_space=pltpu.HBM)] * outside + [spec] * (len(operands) - outside),
        out_specs=out_specs,
        scratch_shapes=list(scratch),
        cost_estimate=pl.CostEstimate(flops=flops, bytes_accessed=moved, transcendentals=0),
        compiler_params=pltpu.CompilerParams(vmem_limit_bytes=limit * 1024 * 1024),
    )(*operands)


def norm_rows(values):
    width = values.shape[0]
    shifted = values - jnp.sum(values, axis=0, keepdims=True) * (1.0 / width)
    variance = jnp.sum(shifted * shifted, axis=0, keepdims=True) * (1.0 / width)
    inv_std = lax.rsqrt(variance + EPS)
    return shifted * inv_std, inv_std


def put_row(ref, i, rows, values):
    for h in range(ref.shape[0]):
        spots = pl.ds(i, values.shape[0], stride=rows)
        ref[h, spots, :] = values[:, h * LANES : (h + 1) * LANES]


def take_row(ref, i, rows):
    spots = pl.ds(i, ref.shape[1] // rows, stride=rows)
    return jnp.concatenate([ref[h, spots, :] for h in range(ref.shape[0])], axis=1)


def fill(got_ref, left_ref, right_ref):
    devices, both, _ = got_ref.shape
    half = both // 2
    for n, ref in enumerate((left_ref, right_ref)):
        for h in range(ref.shape[0]):
            block = got_ref[:, n * half : (n + 1) * half, h * LANES : (h + 1) * LANES]
            ref[h] = block.astype(F32).reshape(devices * half, LANES)


def edges_kernel(
    pair_hbm, gain_hbm, weight_hbm, sent_ref, left_ref, right_ref, pair_ref, gain_ref, weight_ref, sems
):
    rows, res, width = pair_ref.shape
    devices = sent_ref.shape[0]
    half = sent_ref.shape[1] // 2
    pairs = ((weight_hbm, weight_ref), (gain_hbm, gain_ref), (pair_hbm, pair_ref))
    copies = [
        pltpu.make_async_copy(source, target, sems.at[n])
        for n, (source, target) in enumerate(pairs)
    ]
    for copy in copies:
        copy.start()
    copies[0].wait()
    weight = weight_ref[:, : 4 * width].astype(F32).T.astype(BF16)
    copies[1].wait()
    gain = gain_ref[...].T
    copies[2].wait()
    for i in range(rows):
        centred, _ = norm_rows(pair_ref[i].astype(F32).T)
        normed = (centred * gain).astype(BF16)
        out = jnp.dot(weight, normed, preferred_element_type=F32)
        put_row(left_ref, i, rows, jax.nn.sigmoid(out[width : 2 * width]) * out[:width])
        put_row(right_ref, i, rows, jax.nn.sigmoid(out[3 * width :]) * out[2 * width : 3 * width])
    for n, ref in enumerate((left_ref, right_ref)):
        for h in range(res // LANES):
            block = ref[h].reshape(devices, half, LANES).astype(BF16)
            sent_ref[:, n * half : (n + 1) * half, h * LANES : (h + 1) * LANES] = block


def prepare_kernel(
    pair_ref,
    cot_ref,
    gain_in_ref,
    gain_out_ref,
    weight_ref,
    w_out_ref,
    normed_ref,
    factor_ref,
    grad_out_ref,
    scaled_ref,
):
    rows, res, width = pair_ref.shape
    weight = weight_ref[...].astype(F32).T.astype(BF16)
    w_out = w_out_ref[...]
    gain_in, gain_out = gain_in_ref[...].T, gain_out_ref[...].T
    for i in range(rows):
        centred, _ = norm_rows(pair_ref[i].astype(F32).T)
        normed = (centred * gain_in).astype(BF16)
        normed_ref[i] = normed
        out = jnp.dot(weight, normed, preferred_element_type=F32)
        for side in range(2):
            first = 2 * side * width
            sig = jax.nn.sigmoid(out[first + width : first + 2 * width])
            factor_ref[i, first : first + width, :] = sig
            factor_ref[i, first + width : first + 2 * width, :] = (
                out[first : first + width] * sig * (1.0 - sig)
            )
        gate = jax.nn.sigmoid(out[4 * width :])
        factor_ref[i, 4 * width :, :] = gate
        grad_out = (cot_ref[i].astype(F32).T * gate).astype(BF16)
        grad_out_ref[i] = grad_out
        scaled = jnp.dot(w_out, grad_out, preferred_element_type=F32) * gain_out
        scaled = scaled - jnp.sum(scaled, axis=0, keepdims=True) * (1.0 / width)
        put_row(scaled_ref, i, rows, scaled)


def matrices_of(ref, first, share, rows):
    devices, _, res = ref.shape
    block = ref[:, first : first + share * rows, :].astype(F32)
    block = block.reshape(devices, share, rows, res)
    return [block[:, c].reshape(devices * rows, res).astype(BF16) for c in range(share)]


def store_matrices(ref, first, values, rows):
    devices, _, res = ref.shape
    block = jnp.stack([v.reshape(devices, rows, res) for v in values], axis=1)
    ref[:, first : first + len(values) * rows, :] = block.reshape(
        devices, len(values) * rows, res
    ).astype(BF16)


def triangle_kernel(share, rows, got_ref, sent_ref, left_ref, right_ref):
    half = share * rows
    left = matrices_of(got_ref, 0, share, rows)
    right = matrices_of(got_ref, half, share, rows)
    for c in range(share):
        left_ref[c] = left[c]
        right_ref[c] = right[c]
    out = [lax.dot_general(a, b, NT, preferred_element_type=F32) for a, b in zip(left, right)]
    store_matrices(sent_ref, 0, out, rows)


def norm_grad_kernel(rows, got_ref, scaled_ref, sent_ref):
    devices, block, res = got_ref.shape
    share = block // rows
    width = devices * share

    def over_share(values):
        return jnp.sum(values.reshape(share, rows, res), axis=0)

    zero = jnp.zeros((rows, res), F32)

    def scaled_of(d):
        spots = pl.ds(pl.multiple_of(d * block, block), block)
        return jnp.concatenate([scaled_ref[h, spots, :] for h in range(res // LANES)], axis=1)

    def add_up(d, carry):
        return carry + over_share(got_ref[d].astype(F32))

    mean = lax.fori_loop(0, devices, add_up, zero, unroll=4) * (1.0 / width)
    mean = jnp.concatenate([mean] * share, axis=0)

    def second(d, carry):
        shifted = got_ref[d].astype(F32) - mean
        return (
            carry[0] + over_share(shifted * shifted),
            carry[1] + over_share(shifted * scaled_of(d)),
        )

    variance, product = lax.fori_loop(0, devices, second, (zero, zero), unroll=4)
    inv_std = lax.rsqrt(variance * (1.0 / width) + EPS)
    product = product * (1.0 / width) * inv_std * inv_std * inv_std
    inv_std = jnp.concatenate([inv_std] * share, axis=0)
    product = jnp.concatenate([product] * share, axis=0)

    def write(d, carry):
        shifted = got_ref[d].astype(F32) - mean
        sent_ref[d] = (inv_std * scaled_of(d) - shifted * product).astype(BF16)
        return carry

    lax.fori_loop(0, devices, write, 0, unroll=4)


def edge_grads_kernel(share, rows, got_ref, left_ref, right_ref, sent_ref):
    grads = matrices_of(got_ref, 0, share, rows)
    left_grads, right_grads = [], []
    for c in range(share):
        left_grads.append(jnp.dot(grads[c], right_ref[c], preferred_element_type=F32))
        turned = grads[c].astype(F32).T.astype(BF16)
        right_grads.append(jnp.dot(turned, left_ref[c], preferred_element_type=F32))
    store_matrices(sent_ref, 0, left_grads, rows)
    store_matrices(sent_ref, share * rows, right_grads, rows)


def turn(triangle_ref, turned_ref):
    devices, half, _ = triangle_ref.shape
    for h in range(turned_ref.shape[0]):
        block = triangle_ref[:, :, h * LANES : (h + 1) * LANES]
        turned_ref[h] = block.astype(F32).reshape(devices * half, LANES)


def gate_grads(i, rows, factor_ref, cot_ref, gain_out, w_out, turned_ref):
    width = w_out.shape[0]
    centred, _ = norm_rows(take_row(turned_ref, i, rows))
    out_normed = (centred * gain_out).astype(BF16)
    gate = factor_ref[i, 4 * width :, :]
    update = gate * jnp.dot(w_out, out_normed, preferred_element_type=F32)
    grad_gate = (cot_ref[i].astype(F32).T * update * (1.0 - gate)).astype(BF16)
    return out_normed, update, grad_gate


def edge_parts(i, rows, factor_ref, left_ref, right_ref):
    left, right = take_row(left_ref, i, rows), take_row(right_ref, i, rows)
    width = left.shape[0]
    return [
        (grad * factor_ref[i, b * width : (b + 1) * width, :]).astype(BF16)
        for b, grad in enumerate((left, left, right, right))
    ]


def weight_grads_kernel(
    got_ref,
    factor_ref,
    normed_ref,
    triangle_ref,
    cot_ref,
    grad_out_ref,
    gain_out_ref,
    w_out_ref,
    sent_ref,
    left_ref,
    right_ref,
    turned_ref,
):
    rows = normed_ref.shape[0]
    fill(got_ref, left_ref, right_ref)
    turn(triangle_ref, turned_ref)
    w_out = w_out_ref[...].astype(F32).T.astype(BF16)
    gain_out = gain_out_ref[...].T
    total = None
    for i in range(rows):
        out_normed, _, grad_gate = gate_grads(
            i, rows, factor_ref, cot_ref, gain_out, w_out, turned_ref
        )
        grads = edge_parts(i, rows, factor_ref, left_ref, right_ref) + [grad_gate]
        pairs = [(normed_ref[i], grad) for grad in grads] + [(out_normed, grad_out_ref[i])]
        parts = [lax.dot_general(x, y, NT, preferred_element_type=F32) for x, y in pairs]
        total = parts if total is None else [x + y for x, y in zip(total, parts)]
    sent_ref[...] = jnp.concatenate(total, axis=0).reshape(sent_ref.shape).astype(BF16)


def pair_grad_kernel(
    got_ref,
    factor_ref,
    pair_ref,
    triangle_ref,
    cot_ref,
    gain_in_ref,
    gain_out_ref,
    weight_ref,
    w_out_ref,
    out_ref,
    update_ref,
    left_ref,
    right_ref,
    turned_ref,
):
    rows, _, width = pair_ref.shape
    fill(got_ref, left_ref, right_ref)
    turn(triangle_ref, turned_ref)
    weight = weight_ref[...]
    w_out = w_out_ref[...].astype(F32).T.astype(BF16)
    gain_in, gain_out = gain_in_ref[...].T, gain_out_ref[...].T
    for i in range(rows):
        _, update, grad_gate = gate_grads(
            i, rows, factor_ref, cot_ref, gain_out, w_out, turned_ref
        )
        update_ref[i] = update.T.astype(BF16)
        grads = edge_parts(i, rows, factor_ref, left_ref, right_ref) + [grad_gate]
        grads = jnp.concatenate(grads, axis=0)
        scaled = jnp.dot(weight, grads, preferred_element_type=F32) * gain_in
        centred, inv_std = norm_rows(pair_ref[i].astype(F32).T)
        first = jnp.sum(scaled, axis=0, keepdims=True) * (1.0 / width)
        second = jnp.sum(scaled * centred, axis=0, keepdims=True) * (1.0 / width)
        grad_pair = inv_std * (scaled - first - centred * second)
        out_ref[i] = grad_pair.T.astype(BF16)


def finish_kernel(full_ref, weight_ref, w_out_ref, gain_in_ref, gain_out_ref, *outs):
    grad_weight_ref, grad_out_ref, grad_gain_in_ref, grad_gain_out_ref = outs
    width = w_out_ref.shape[0]
    full = full_ref[...].astype(F32).reshape(6 * width, width)
    weight = weight_ref[...].astype(F32)
    total = jnp.zeros((width, width), F32)
    for b in range(5):
        block = full[b * width : (b + 1) * width]
        grad_weight_ref[:, b * width : (b + 1) * width] = block
        total = total + block * weight[:, b * width : (b + 1) * width]
    block = full[5 * width :]
    grad_out_ref[...] = block
    total_out = block * w_out_ref[...].astype(F32)
    grad_gain_in_ref[...] = jnp.sum(total.T, axis=0, keepdims=True) / gain_in_ref[...]
    grad_gain_out_ref[...] = jnp.sum(total_out.T, axis=0, keepdims=True) / gain_out_ref[...]


def local(devices, pair, gain_in, w_proj, gain_out, w_out, cotangent):
    width = gain_out.shape[0]
    rows, res, _ = pair.shape
    share = width // devices
    half = share * rows
    shape = jax.ShapeDtypeStruct
    scratch = [pltpu.VMEM((res // LANES, width * rows, LANES), F32)] * 2

    sent = call(
        edges_kernel,
        shape((devices, 2 * half, res), BF16),
        (pair, gain_in[None], w_proj),
        scratch
        + [pltpu.VMEM(pair.shape, BF16), pltpu.VMEM((1, width), F32)]
        + [pltpu.VMEM(w_proj.shape, BF16), pltpu.SemaphoreType.DMA((3,))],
        outside=3,
        limit=62,
    )
    sent, pair, cotangent = hold(sent, pair, cotangent)
    got = exchange(sent)

    turned = shape((rows, width, res), BF16)
    normed, factor, grad_proj_out, scaled = call(
        prepare_kernel,
        (
            turned,
            shape((rows, 5 * width, res), F32),
            turned,
            shape((res // LANES, width * rows, LANES), F32),
        ),
        (pair, cotangent, gain_in[None], gain_out[None], w_proj, w_out),
        flops=2 * rows * res * width * 6 * width,
    )
    got, normed, factor, grad_proj_out, scaled = hold(got, normed, factor, grad_proj_out, scaled)
    edge = shape((share, devices * rows, res), BF16)
    sent, left, right = call(
        functools.partial(triangle_kernel, share, rows),
        (shape((devices, half, res), BF16), edge, edge),
        (got,),
    )
    triangle = exchange(sent)
    sent = call(
        functools.partial(norm_grad_kernel, rows),
        shape((devices, half, res), BF16),
        (triangle, scaled),
    )
    got = exchange(sent)
    sent = call(
        functools.partial(edge_grads_kernel, share, rows),
        shape((devices, 2 * half, res), BF16),
        (got, left, right),
    )
    got = exchange(sent)
    sent = call(
        weight_grads_kernel,
        shape((devices, 6 * width // devices, width), BF16),
        (got, factor, normed, triangle, cotangent, grad_proj_out, gain_out[None], w_out),
        scratch + scratch[:1],
    )
    sums = exchange(sent)
    mine = jnp.sum(sums.astype(F32), axis=0).astype(BF16)
    mine = jnp.broadcast_to(mine[None], (devices,) + mine.shape)
    mine, edge_grads, factor, triangle = hold(mine, got, factor, triangle)
    full = exchange(mine)
    grad_pair, update = call(
        pair_grad_kernel,
        [shape((rows, res, width), BF16)] * 2,
        (edge_grads, factor, pair, triangle, cotangent)
        + (gain_in[None], gain_out[None], w_proj, w_out),
        scratch + scratch[:1],
        flops=2 * rows * res * width * 6 * width,
    )
    grad_w_proj, grad_w_out, grad_gain_in, grad_gain_out = call(
        finish_kernel,
        (
            shape((width, 5 * width), F32),
            shape((width, width), F32),
            shape((1, width), F32),
            shape((1, width), F32),
        ),
        (full, w_proj, w_out, gain_in[None], gain_out[None]),
    )
    return (update, grad_pair, grad_gain_in[0], grad_w_proj, grad_gain_out[0], grad_w_out)


def solution(mesh):
    devices = mesh.shape["dap"]

    def program(*args):
        return local(devices, *args)

    in_specs = (P(("dp", "dap"), None, None), P(), P(), P(), P(), P(("dp", "dap"), None, None))
    out_specs = (
        P(("dp", "dap"), None, None),
        P(("dp", "dap"), None, None),
        P("dp"),
        P("dp", None),
        P("dp"),
        P("dp", None),
    )
    return jax.shard_map(program, mesh=mesh, in_specs=in_specs, out_specs=out_specs, check_vma=False)
```

```python
import functools

import jax
import jax.numpy as jnp
from jax import lax
from jax.experimental import pallas as pl
from jax.experimental.pallas import tpu as pltpu
from jax.sharding import PartitionSpec as P

F32, BF16 = jnp.float32, jnp.bfloat16
EPS = 1e-05
LANES = 128
NT = (((1,), (1,)), ((), ()))


def places(devices):
    if devices % 16:
        return list(range(devices))
    order = []
    for high in range(0, devices, 16):
        for core in range(2):
            order += [high + 2 * z + core for z in (0, 2, 4, 6, 1, 3, 5, 7)]
    return order


def exchange(values):
    groups = [places(values.shape[0])]
    return lax.all_to_all(values, "dap", 0, 0, tiled=True, axis_index_groups=groups)


def hold(*values):
    return lax.optimization_barrier(values)


def call(kernel, out_shape, operands, scratch=(), flops=0, outside=0, limit=16):
    leaves = out_shape if isinstance(out_shape, (tuple, list)) else [out_shape]
    moved = sum(a.size * a.dtype.itemsize for a in list(operands) + list(leaves))
    spec = pl.BlockSpec(memory_space=pltpu.VMEM)
    out_specs = [spec] * len(out_shape) if isinstance(out_shape, (tuple, list)) else spec
    return pl.pallas_call(
        kernel,
        out_shape=out_shape,
        in_specs=[pl.BlockSpec(memory_space=pltpu.HBM)] * outside + [spec] * (len(operands) - outside),
        out_specs=out_specs,
        scratch_shapes=list(scratch),
        cost_estimate=pl.CostEstimate(flops=flops, bytes_accessed=moved, transcendentals=0),
        compiler_params=pltpu.CompilerParams(vmem_limit_bytes=limit * 1024 * 1024),
    )(*operands)


def norm_rows(values):
    width = values.shape[0]
    shifted = values - jnp.sum(values, axis=0, keepdims=True) * (1.0 / width)
    variance = jnp.sum(shifted * shifted, axis=0, keepdims=True) * (1.0 / width)
    inv_std = lax.rsqrt(variance + EPS)
    return shifted * inv_std, inv_std


def put_row(ref, i, rows, values):
    for h in range(ref.shape[0]):
        spots = pl.ds(i, values.shape[0], stride=rows)
        ref[h, spots, :] = values[:, h * LANES : (h + 1) * LANES]


def take_row(ref, i, rows):
    spots = pl.ds(i, ref.shape[1] // rows, stride=rows)
    return jnp.concatenate([ref[h, spots, :] for h in range(ref.shape[0])], axis=1)


def fill(got_ref, left_ref, right_ref):
    devices, both, _ = got_ref.shape
    half = both // 2
    for n, ref in enumerate((left_ref, right_ref)):
        for h in range(ref.shape[0]):
            block = got_ref[:, n * half : (n + 1) * half, h * LANES : (h + 1) * LANES]
            ref[h] = block.astype(F32).reshape(devices * half, LANES)


def edges_kernel(
    pair_hbm, gain_hbm, weight_hbm, sent_ref, left_ref, right_ref, pair_ref, gain_ref, weight_ref, sems
):
    rows, res, width = pair_ref.shape
    devices = sent_ref.shape[0]
    half = sent_ref.shape[1] // 2
    pairs = ((weight_hbm, weight_ref), (gain_hbm, gain_ref), (pair_hbm, pair_ref))
    copies = [
        pltpu.make_async_copy(source, target, sems.at[n])
        for n, (source, target) in enumerate(pairs)
    ]
    for copy in copies:
        copy.start()
    copies[0].wait()
    weight = weight_ref[:, : 4 * width].astype(F32).T.astype(BF16)
    copies[1].wait()
    gain = gain_ref[...].T
    copies[2].wait()
    for i in range(rows):
        centred, _ = norm_rows(pair_ref[i].astype(F32).T)
        normed = (centred * gain).astype(BF16)
        out = jnp.dot(weight, normed, preferred_element_type=F32)
        put_row(left_ref, i, rows, jax.nn.sigmoid(out[width : 2 * width]) * out[:width])
        put_row(right_ref, i, rows, jax.nn.sigmoid(out[3 * width :]) * out[2 * width : 3 * width])
    for n, ref in enumerate((left_ref, right_ref)):
        for h in range(res // LANES):
            block = ref[h].reshape(devices, half, LANES).astype(BF16)
            sent_ref[:, n * half : (n + 1) * half, h * LANES : (h + 1) * LANES] = block


def prepare_kernel(
    pair_ref,
    cot_ref,
    gain_in_ref,
    gain_out_ref,
    weight_ref,
    w_out_ref,
    normed_ref,
    factor_ref,
    grad_out_ref,
    scaled_ref,
):
    rows, res, width = pair_ref.shape
    weight = weight_ref[...].astype(F32).T.astype(BF16)
    w_out = w_out_ref[...]
    gain_in, gain_out = gain_in_ref[...].T, gain_out_ref[...].T
    for i in range(rows):
        centred, _ = norm_rows(pair_ref[i].astype(F32).T)
        normed = (centred * gain_in).astype(BF16)
        normed_ref[i] = normed
        out = jnp.dot(weight, normed, preferred_element_type=F32)
        for side in range(2):
            first = 2 * side * width
            sig = jax.nn.sigmoid(out[first + width : first + 2 * width])
            factor_ref[i, first : first + width, :] = sig
            factor_ref[i, first + width : first + 2 * width, :] = (
                out[first : first + width] * sig * (1.0 - sig)
            )
        gate = jax.nn.sigmoid(out[4 * width :])
        factor_ref[i, 4 * width :, :] = gate
        grad_out = (cot_ref[i].astype(F32).T * gate).astype(BF16)
        grad_out_ref[i] = grad_out
        scaled = jnp.dot(w_out, grad_out, preferred_element_type=F32) * gain_out
        scaled = scaled - jnp.sum(scaled, axis=0, keepdims=True) * (1.0 / width)
        put_row(scaled_ref, i, rows, scaled)


def reorder(block, order):
    return jnp.stack([block[m] for m in order], axis=0)


def matrices_of(ref, first, share, rows, in_order=False):
    devices, _, res = ref.shape
    block = ref[:, first : first + share * rows, :].astype(F32)
    if in_order:
        order = places(devices)
        block = reorder(block, [order.index(d) for d in range(devices)])
    block = block.reshape(devices, share, rows, res)
    return [block[:, c].reshape(devices * rows, res).astype(BF16) for c in range(share)]


def store_matrices(ref, first, values, rows, in_order=False):
    devices, _, res = ref.shape
    block = jnp.stack([v.reshape(devices, rows, res) for v in values], axis=1)
    if in_order:
        block = reorder(block, places(devices))
    ref[:, first : first + len(values) * rows, :] = block.reshape(
        devices, len(values) * rows, res
    ).astype(BF16)


def triangle_kernel(share, rows, got_ref, sent_ref, left_ref, right_ref):
    half = share * rows
    left = matrices_of(got_ref, 0, share, rows)
    right = matrices_of(got_ref, half, share, rows, in_order=True)
    for c in range(share):
        left_ref[c] = left[c]
        right_ref[c] = right[c]
    out = [lax.dot_general(a, b, NT, preferred_element_type=F32) for a, b in zip(left, right)]
    store_matrices(sent_ref, 0, out, rows)


def norm_grad_kernel(rows, got_ref, scaled_ref, sent_ref):
    devices, block, res = got_ref.shape
    share = block // rows
    width = devices * share

    def over_share(values):
        return jnp.sum(values.reshape(share, rows, res), axis=0)

    zero = jnp.zeros((rows, res), F32)

    def scaled_of(d):
        spots = pl.ds(pl.multiple_of(d * block, block), block)
        return jnp.concatenate([scaled_ref[h, spots, :] for h in range(res // LANES)], axis=1)

    def add_up(d, carry):
        return carry + over_share(got_ref[d].astype(F32))

    mean = lax.fori_loop(0, devices, add_up, zero, unroll=4) * (1.0 / width)
    mean = jnp.concatenate([mean] * share, axis=0)

    def second(d, carry):
        shifted = got_ref[d].astype(F32) - mean
        return (
            carry[0] + over_share(shifted * shifted),
            carry[1] + over_share(shifted * scaled_of(d)),
        )

    variance, product = lax.fori_loop(0, devices, second, (zero, zero), unroll=4)
    inv_std = lax.rsqrt(variance * (1.0 / width) + EPS)
    product = product * (1.0 / width) * inv_std * inv_std * inv_std
    inv_std = jnp.concatenate([inv_std] * share, axis=0)
    product = jnp.concatenate([product] * share, axis=0)

    def write(d, carry):
        shifted = got_ref[d].astype(F32) - mean
        sent_ref[d] = (inv_std * scaled_of(d) - shifted * product).astype(BF16)
        return carry

    lax.fori_loop(0, devices, write, 0, unroll=4)


def edge_grads_kernel(share, rows, got_ref, left_ref, right_ref, sent_ref):
    grads = matrices_of(got_ref, 0, share, rows)
    left_grads, right_grads = [], []
    for c in range(share):
        left_grads.append(jnp.dot(grads[c], right_ref[c], preferred_element_type=F32))
        turned = grads[c].astype(F32).T.astype(BF16)
        right_grads.append(jnp.dot(turned, left_ref[c], preferred_element_type=F32))
    store_matrices(sent_ref, 0, left_grads, rows)
    store_matrices(sent_ref, share * rows, right_grads, rows, in_order=True)


def turn(triangle_ref, turned_ref):
    devices, half, _ = triangle_ref.shape
    for h in range(turned_ref.shape[0]):
        block = triangle_ref[:, :, h * LANES : (h + 1) * LANES]
        turned_ref[h] = block.astype(F32).reshape(devices * half, LANES)


def gate_grads(i, rows, factor_ref, cot_ref, gain_out, w_out, turned_ref):
    width = w_out.shape[0]
    centred, _ = norm_rows(take_row(turned_ref, i, rows))
    out_normed = (centred * gain_out).astype(BF16)
    gate = factor_ref[i, 4 * width :, :]
    update = gate * jnp.dot(w_out, out_normed, preferred_element_type=F32)
    grad_gate = (cot_ref[i].astype(F32).T * update * (1.0 - gate)).astype(BF16)
    return out_normed, update, grad_gate


def edge_parts(i, rows, factor_ref, left_ref, right_ref):
    left, right = take_row(left_ref, i, rows), take_row(right_ref, i, rows)
    width = left.shape[0]
    return [
        (grad * factor_ref[i, b * width : (b + 1) * width, :]).astype(BF16)
        for b, grad in enumerate((left, left, right, right))
    ]


def weight_grads_kernel(
    got_ref,
    factor_ref,
    normed_ref,
    triangle_ref,
    cot_ref,
    grad_out_ref,
    gain_out_ref,
    w_out_ref,
    sent_ref,
    left_ref,
    right_ref,
    turned_ref,
):
    rows = normed_ref.shape[0]
    fill(got_ref, left_ref, right_ref)
    turn(triangle_ref, turned_ref)
    w_out = w_out_ref[...].astype(F32).T.astype(BF16)
    gain_out = gain_out_ref[...].T
    total = None
    for i in range(rows):
        out_normed, _, grad_gate = gate_grads(
            i, rows, factor_ref, cot_ref, gain_out, w_out, turned_ref
        )
        grads = edge_parts(i, rows, factor_ref, left_ref, right_ref) + [grad_gate]
        pairs = [(normed_ref[i], grad) for grad in grads] + [(out_normed, grad_out_ref[i])]
        parts = [lax.dot_general(x, y, NT, preferred_element_type=F32) for x, y in pairs]
        total = parts if total is None else [x + y for x, y in zip(total, parts)]
    sent_ref[...] = jnp.concatenate(total, axis=0).reshape(sent_ref.shape).astype(BF16)


def pair_grad_kernel(
    got_ref,
    factor_ref,
    pair_ref,
    triangle_ref,
    cot_ref,
    gain_in_ref,
    gain_out_ref,
    weight_ref,
    w_out_ref,
    out_ref,
    update_ref,
    left_ref,
    right_ref,
    turned_ref,
):
    rows, _, width = pair_ref.shape
    fill(got_ref, left_ref, right_ref)
    turn(triangle_ref, turned_ref)
    weight = weight_ref[...]
    w_out = w_out_ref[...].astype(F32).T.astype(BF16)
    gain_in, gain_out = gain_in_ref[...].T, gain_out_ref[...].T
    for i in range(rows):
        _, update, grad_gate = gate_grads(
            i, rows, factor_ref, cot_ref, gain_out, w_out, turned_ref
        )
        update_ref[i] = update.T.astype(BF16)
        grads = edge_parts(i, rows, factor_ref, left_ref, right_ref) + [grad_gate]
        grads = jnp.concatenate(grads, axis=0)
        scaled = jnp.dot(weight, grads, preferred_element_type=F32) * gain_in
        centred, inv_std = norm_rows(pair_ref[i].astype(F32).T)
        first = jnp.sum(scaled, axis=0, keepdims=True) * (1.0 / width)
        second = jnp.sum(scaled * centred, axis=0, keepdims=True) * (1.0 / width)
        grad_pair = inv_std * (scaled - first - centred * second)
        out_ref[i] = grad_pair.T.astype(BF16)


def finish_kernel(full_ref, weight_ref, w_out_ref, gain_in_ref, gain_out_ref, *outs):
    grad_weight_ref, grad_out_ref, grad_gain_in_ref, grad_gain_out_ref = outs
    width = w_out_ref.shape[0]
    full = full_ref[...].astype(F32).reshape(6 * width, width)
    weight = weight_ref[...].astype(F32)
    total = jnp.zeros((width, width), F32)
    for b in range(5):
        block = full[b * width : (b + 1) * width]
        grad_weight_ref[:, b * width : (b + 1) * width] = block
        total = total + block * weight[:, b * width : (b + 1) * width]
    block = full[5 * width :]
    grad_out_ref[...] = block
    total_out = block * w_out_ref[...].astype(F32)
    grad_gain_in_ref[...] = jnp.sum(total.T, axis=0, keepdims=True) / gain_in_ref[...]
    grad_gain_out_ref[...] = jnp.sum(total_out.T, axis=0, keepdims=True) / gain_out_ref[...]


def local(devices, pair, gain_in, w_proj, gain_out, w_out, cotangent):
    width = gain_out.shape[0]
    rows, res, _ = pair.shape
    share = width // devices
    half = share * rows
    shape = jax.ShapeDtypeStruct
    scratch = [pltpu.VMEM((res // LANES, width * rows, LANES), F32)] * 2

    sent = call(
        edges_kernel,
        shape((devices, 2 * half, res), BF16),
        (pair, gain_in[None], w_proj),
        scratch
        + [pltpu.VMEM(pair.shape, BF16), pltpu.VMEM((1, width), F32)]
        + [pltpu.VMEM(w_proj.shape, BF16), pltpu.SemaphoreType.DMA((3,))],
        outside=3,
        limit=62,
    )
    sent, pair, cotangent = hold(sent, pair, cotangent)
    got = exchange(sent)

    turned = shape((rows, width, res), BF16)
    normed, factor, grad_proj_out, scaled = call(
        prepare_kernel,
        (
            turned,
            shape((rows, 5 * width, res), F32),
            turned,
            shape((res // LANES, width * rows, LANES), F32),
        ),
        (pair, cotangent, gain_in[None], gain_out[None], w_proj, w_out),
        flops=2 * rows * res * width * 6 * width,
    )
    got, normed, factor, grad_proj_out, scaled = hold(got, normed, factor, grad_proj_out, scaled)
    edge = shape((share, devices * rows, res), BF16)
    sent, left, right = call(
        functools.partial(triangle_kernel, share, rows),
        (shape((devices, half, res), BF16), edge, edge),
        (got,),
    )
    triangle = exchange(sent)
    sent = call(
        functools.partial(norm_grad_kernel, rows),
        shape((devices, half, res), BF16),
        (triangle, scaled),
    )
    got = exchange(sent)
    sent = call(
        functools.partial(edge_grads_kernel, share, rows),
        shape((devices, 2 * half, res), BF16),
        (got, left, right),
    )
    got = exchange(sent)
    sent = call(
        weight_grads_kernel,
        shape((devices, 6 * width // devices, width), BF16),
        (got, factor, normed, triangle, cotangent, grad_proj_out, gain_out[None], w_out),
        scratch + scratch[:1],
    )
    sums = exchange(sent)
    mine = jnp.sum(sums.astype(F32), axis=0).astype(BF16)
    mine = jnp.broadcast_to(mine[None], (devices,) + mine.shape)
    mine, edge_grads, factor, triangle = hold(mine, got, factor, triangle)
    full = exchange(mine)
    grad_pair, update = call(
        pair_grad_kernel,
        [shape((rows, res, width), BF16)] * 2,
        (edge_grads, factor, pair, triangle, cotangent)
        + (gain_in[None], gain_out[None], w_proj, w_out),
        scratch + scratch[:1],
        flops=2 * rows * res * width * 6 * width,
    )
    grad_w_proj, grad_w_out, grad_gain_in, grad_gain_out = call(
        finish_kernel,
        (
            shape((width, 5 * width), F32),
            shape((width, width), F32),
            shape((1, width), F32),
            shape((1, width), F32),
        ),
        (full, w_proj, w_out, gain_in[None], gain_out[None]),
    )
    return (update, grad_pair, grad_gain_in[0], grad_w_proj, grad_gain_out[0], grad_w_out)


def solution(mesh):
    devices = mesh.shape["dap"]

    def program(*args):
        return local(devices, *args)

    in_specs = (P(("dp", "dap"), None, None), P(), P(), P(), P(), P(("dp", "dap"), None, None))
    out_specs = (
        P(("dp", "dap"), None, None),
        P(("dp", "dap"), None, None),
        P("dp"),
        P("dp", None),
        P("dp"),
        P("dp", None),
    )
    return jax.shard_map(program, mesh=mesh, in_specs=in_specs, out_specs=out_specs, check_vma=False)
```

```python
import functools

import jax
import jax.numpy as jnp
from jax import lax
from jax.experimental import pallas as pl
from jax.experimental.pallas import tpu as pltpu
from jax.sharding import PartitionSpec as P

F32, BF16 = jnp.float32, jnp.bfloat16
EPS = 1e-05
LANES = 128
PIECES = 4
NT = (((1,), (1,)), ((), ()))


def places(devices):
    if devices % 16:
        return list(range(devices))
    order = []
    for n, high in enumerate(range(0, devices, 16)):
        for core in (n % 2, 1 - n % 2):
            order += [high + 2 * z + core for z in (0, 3, 4, 7, 1, 2, 5, 6)]
    return order


def exchange(values):
    groups = [places(values.shape[0])]
    return lax.all_to_all(values, "dap", 0, 0, tiled=True, axis_index_groups=groups)


def hold(*values):
    return lax.optimization_barrier(values)


def call(kernel, out_shape, operands, scratch=(), flops=0, outside=0, limit=16, leave=False):
    leaves = out_shape if isinstance(out_shape, (tuple, list)) else [out_shape]
    moved = sum(a.size * a.dtype.itemsize for a in list(operands) + list(leaves))
    spec = pl.BlockSpec(memory_space=pltpu.VMEM)
    if leave:
        out_specs = pl.BlockSpec(memory_space=pl.ANY)
    else:
        out_specs = [spec] * len(out_shape) if isinstance(out_shape, (tuple, list)) else spec
    return pl.pallas_call(
        kernel,
        out_shape=out_shape,
        in_specs=[pl.BlockSpec(memory_space=pltpu.HBM)] * outside + [spec] * (len(operands) - outside),
        out_specs=out_specs,
        scratch_shapes=list(scratch),
        cost_estimate=pl.CostEstimate(flops=flops, bytes_accessed=moved, transcendentals=0),
        compiler_params=pltpu.CompilerParams(vmem_limit_bytes=limit * 1024 * 1024),
    )(*operands)


def norm_rows(values):
    width = values.shape[0]
    shifted = values - jnp.sum(values, axis=0, keepdims=True) * (1.0 / width)
    variance = jnp.sum(shifted * shifted, axis=0, keepdims=True) * (1.0 / width)
    inv_std = lax.rsqrt(variance + EPS)
    return shifted * inv_std, inv_std


def put_row(ref, i, rows, values):
    for h in range(ref.shape[0]):
        spots = pl.ds(i, values.shape[0], stride=rows)
        ref[h, spots, :] = values[:, h * LANES : (h + 1) * LANES]


def take_row(ref, i, rows):
    spots = pl.ds(i, ref.shape[1] // rows, stride=rows)
    return jnp.concatenate([ref[h, spots, :] for h in range(ref.shape[0])], axis=1)


def fill(got_ref, left_ref, right_ref):
    devices, both, _ = got_ref.shape
    half = both // 2
    for n, ref in enumerate((left_ref, right_ref)):
        for h in range(ref.shape[0]):
            block = got_ref[:, n * half : (n + 1) * half, h * LANES : (h + 1) * LANES]
            ref[h] = block.astype(F32).reshape(devices * half, LANES)


def edges_kernel(
    pair_hbm, gain_hbm, weight_hbm, sent_hbm, left_ref, right_ref, pair_ref, gain_ref, weight_ref, sent_ref, sems
):
    rows, res, width = pair_ref.shape
    devices = sent_ref.shape[0]
    half = sent_ref.shape[1] // 2
    pairs = ((weight_hbm, weight_ref), (gain_hbm, gain_ref), (pair_hbm, pair_ref))
    copies = [
        pltpu.make_async_copy(source, target, sems.at[n])
        for n, (source, target) in enumerate(pairs)
    ]
    for copy in copies:
        copy.start()
    copies[0].wait()
    weight = weight_ref[:, : 4 * width].astype(F32).T.astype(BF16)
    copies[1].wait()
    gain = gain_ref[...].T
    copies[2].wait()
    for i in range(rows):
        centred, _ = norm_rows(pair_ref[i].T.astype(F32))
        normed = (centred * gain).astype(BF16)
        out = jnp.dot(weight, normed, preferred_element_type=F32)
        put_row(left_ref, i, rows, jax.nn.sigmoid(out[width : 2 * width]) * out[:width])
        put_row(right_ref, i, rows, jax.nn.sigmoid(out[3 * width :]) * out[2 * width : 3 * width])
    step = devices // PIECES
    copies = []
    for piece in range(PIECES):
        slots = pl.ds(piece * step, step)
        for n, ref in enumerate((left_ref, right_ref)):
            for h in range(res // LANES):
                block = ref[h, pl.ds(piece * step * half, step * half), :]
                block = block.reshape(step, half, LANES).astype(BF16)
                sent_ref[slots, n * half : (n + 1) * half, h * LANES : (h + 1) * LANES] = block
        copy = pltpu.make_async_copy(sent_ref.at[slots], sent_hbm.at[slots], sems.at[3 + piece])
        copy.start()
        copies.append(copy)
    for copy in copies:
        copy.wait()


def prepare_kernel(
    pair_ref,
    cot_ref,
    gain_in_ref,
    gain_out_ref,
    weight_ref,
    w_out_ref,
    normed_ref,
    factor_ref,
    grad_out_ref,
    scaled_ref,
):
    rows, res, width = pair_ref.shape
    weight = weight_ref[...].astype(F32).T.astype(BF16)
    w_out = w_out_ref[...]
    gain_in, gain_out = gain_in_ref[...].T, gain_out_ref[...].T
    for i in range(rows):
        centred, _ = norm_rows(pair_ref[i].astype(F32).T)
        normed = (centred * gain_in).astype(BF16)
        normed_ref[i] = normed
        out = jnp.dot(weight, normed, preferred_element_type=F32)
        for side in range(2):
            first = 2 * side * width
            sig = jax.nn.sigmoid(out[first + width : first + 2 * width])
            factor_ref[i, first : first + width, :] = sig
            factor_ref[i, first + width : first + 2 * width, :] = (
                out[first : first + width] * sig * (1.0 - sig)
            )
        gate = jax.nn.sigmoid(out[4 * width :])
        factor_ref[i, 4 * width :, :] = gate
        grad_out = (cot_ref[i].astype(F32).T * gate).astype(BF16)
        grad_out_ref[i] = grad_out
        scaled = jnp.dot(w_out, grad_out, preferred_element_type=F32) * gain_out
        scaled = scaled - jnp.sum(scaled, axis=0, keepdims=True) * (1.0 / width)
        put_row(scaled_ref, i, rows, scaled)


def reorder(block, order):
    return jnp.stack([block[m] for m in order], axis=0)


def matrices_of(ref, first, share, rows, in_order=False):
    devices, _, res = ref.shape
    block = ref[:, first : first + share * rows, :].astype(F32)
    if in_order:
        order = places(devices)
        block = reorder(block, [order.index(d) for d in range(devices)])
    block = block.reshape(devices, share, rows, res)
    return [block[:, c].reshape(devices * rows, res).astype(BF16) for c in range(share)]


def store_matrices(ref, first, values, rows, in_order=False):
    devices, _, res = ref.shape
    block = jnp.stack([v.reshape(devices, rows, res) for v in values], axis=1)
    if in_order:
        block = reorder(block, places(devices))
    ref[:, first : first + len(values) * rows, :] = block.reshape(
        devices, len(values) * rows, res
    ).astype(BF16)


def triangle_kernel(share, rows, got_ref, sent_ref, left_ref, right_ref):
    half = share * rows
    left = matrices_of(got_ref, 0, share, rows)
    right = matrices_of(got_ref, half, share, rows, in_order=True)
    for c in range(share):
        left_ref[c] = left[c]
        right_ref[c] = right[c]
    out = [lax.dot_general(a, b, NT, preferred_element_type=F32) for a, b in zip(left, right)]
    store_matrices(sent_ref, 0, out, rows)


def norm_grad_kernel(rows, got_ref, scaled_ref, sent_ref):
    devices, block, res = got_ref.shape
    share = block // rows
    width = devices * share

    def over_share(values):
        return jnp.sum(values.reshape(share, rows, res), axis=0)

    zero = jnp.zeros((rows, res), F32)

    def scaled_of(d):
        spots = pl.ds(pl.multiple_of(d * block, block), block)
        return jnp.concatenate([scaled_ref[h, spots, :] for h in range(res // LANES)], axis=1)

    def add_up(d, carry):
        return carry + over_share(got_ref[d].astype(F32))

    mean = lax.fori_loop(0, devices, add_up, zero, unroll=4) * (1.0 / width)
    mean = jnp.concatenate([mean] * share, axis=0)

    def second(d, carry):
        shifted = got_ref[d].astype(F32) - mean
        return (
            carry[0] + over_share(shifted * shifted),
            carry[1] + over_share(shifted * scaled_of(d)),
        )

    variance, product = lax.fori_loop(0, devices, second, (zero, zero), unroll=4)
    inv_std = lax.rsqrt(variance * (1.0 / width) + EPS)
    product = product * (1.0 / width) * inv_std * inv_std * inv_std
    inv_std = jnp.concatenate([inv_std] * share, axis=0)
    product = jnp.concatenate([product] * share, axis=0)

    def write(d, carry):
        shifted = got_ref[d].astype(F32) - mean
        sent_ref[d] = (inv_std * scaled_of(d) - shifted * product).astype(BF16)
        return carry

    lax.fori_loop(0, devices, write, 0, unroll=4)


def edge_grads_kernel(share, rows, got_ref, left_ref, right_ref, sent_ref):
    grads = matrices_of(got_ref, 0, share, rows)
    left_grads, right_grads = [], []
    for c in range(share):
        left_grads.append(jnp.dot(grads[c], right_ref[c], preferred_element_type=F32))
        turned = grads[c].astype(F32).T.astype(BF16)
        right_grads.append(jnp.dot(turned, left_ref[c], preferred_element_type=F32))
    store_matrices(sent_ref, 0, left_grads, rows)
    store_matrices(sent_ref, share * rows, right_grads, rows, in_order=True)


def turn(triangle_ref, turned_ref):
    devices, half, _ = triangle_ref.shape
    for h in range(turned_ref.shape[0]):
        block = triangle_ref[:, :, h * LANES : (h + 1) * LANES]
        turned_ref[h] = block.astype(F32).reshape(devices * half, LANES)


def gate_grads(i, rows, factor_ref, cot_ref, gain_out, w_out, turned_ref):
    width = w_out.shape[0]
    centred, _ = norm_rows(take_row(turned_ref, i, rows))
    out_normed = (centred * gain_out).astype(BF16)
    gate = factor_ref[i, 4 * width :, :]
    update = gate * jnp.dot(w_out, out_normed, preferred_element_type=F32)
    grad_gate = (cot_ref[i].astype(F32).T * update * (1.0 - gate)).astype(BF16)
    return out_normed, update, grad_gate


def edge_parts(i, rows, factor_ref, left_ref, right_ref):
    left, right = take_row(left_ref, i, rows), take_row(right_ref, i, rows)
    width = left.shape[0]
    return [
        (grad * factor_ref[i, b * width : (b + 1) * width, :]).astype(BF16)
        for b, grad in enumerate((left, left, right, right))
    ]


def weight_grads_kernel(
    got_ref,
    factor_ref,
    normed_ref,
    triangle_ref,
    cot_ref,
    grad_out_ref,
    gain_out_ref,
    w_out_ref,
    sent_ref,
    left_ref,
    right_ref,
    turned_ref,
):
    rows = normed_ref.shape[0]
    fill(got_ref, left_ref, right_ref)
    turn(triangle_ref, turned_ref)
    w_out = w_out_ref[...].astype(F32).T.astype(BF16)
    gain_out = gain_out_ref[...].T
    total = None
    for i in range(rows):
        out_normed, _, grad_gate = gate_grads(
            i, rows, factor_ref, cot_ref, gain_out, w_out, turned_ref
        )
        grads = edge_parts(i, rows, factor_ref, left_ref, right_ref) + [grad_gate]
        pairs = [(normed_ref[i], grad) for grad in grads] + [(out_normed, grad_out_ref[i])]
        parts = [lax.dot_general(x, y, NT, preferred_element_type=F32) for x, y in pairs]
        total = parts if total is None else [x + y for x, y in zip(total, parts)]
    sent_ref[...] = jnp.concatenate(total, axis=0).reshape(sent_ref.shape).astype(BF16)


def pair_grad_kernel(
    got_ref,
    factor_ref,
    pair_ref,
    triangle_ref,
    cot_ref,
    gain_in_ref,
    gain_out_ref,
    weight_ref,
    w_out_ref,
    out_ref,
    update_ref,
    left_ref,
    right_ref,
    turned_ref,
):
    rows, _, width = pair_ref.shape
    fill(got_ref, left_ref, right_ref)
    turn(triangle_ref, turned_ref)
    weight = weight_ref[...]
    w_out = w_out_ref[...].astype(F32).T.astype(BF16)
    gain_in, gain_out = gain_in_ref[...].T, gain_out_ref[...].T
    for i in range(rows):
        _, update, grad_gate = gate_grads(
            i, rows, factor_ref, cot_ref, gain_out, w_out, turned_ref
        )
        update_ref[i] = update.T.astype(BF16)
        grads = edge_parts(i, rows, factor_ref, left_ref, right_ref) + [grad_gate]
        grads = jnp.concatenate(grads, axis=0)
        scaled = jnp.dot(weight, grads, preferred_element_type=F32) * gain_in
        centred, inv_std = norm_rows(pair_ref[i].astype(F32).T)
        first = jnp.sum(scaled, axis=0, keepdims=True) * (1.0 / width)
        second = jnp.sum(scaled * centred, axis=0, keepdims=True) * (1.0 / width)
        grad_pair = inv_std * (scaled - first - centred * second)
        out_ref[i] = grad_pair.T.astype(BF16)


def finish_kernel(full_ref, weight_ref, w_out_ref, gain_in_ref, gain_out_ref, *outs):
    grad_weight_ref, grad_out_ref, grad_gain_in_ref, grad_gain_out_ref = outs
    width = w_out_ref.shape[0]
    full = full_ref[...].astype(F32).reshape(6 * width, width)
    weight = weight_ref[...].astype(F32)
    total = jnp.zeros((width, width), F32)
    for b in range(5):
        block = full[b * width : (b + 1) * width]
        grad_weight_ref[:, b * width : (b + 1) * width] = block
        total = total + block * weight[:, b * width : (b + 1) * width]
    block = full[5 * width :]
    grad_out_ref[...] = block
    total_out = block * w_out_ref[...].astype(F32)
    grad_gain_in_ref[...] = jnp.sum(total.T, axis=0, keepdims=True) / gain_in_ref[...]
    grad_gain_out_ref[...] = jnp.sum(total_out.T, axis=0, keepdims=True) / gain_out_ref[...]


def local(devices, pair, gain_in, w_proj, gain_out, w_out, cotangent):
    width = gain_out.shape[0]
    rows, res, _ = pair.shape
    share = width // devices
    half = share * rows
    shape = jax.ShapeDtypeStruct
    scratch = [pltpu.VMEM((res // LANES, width * rows, LANES), F32)] * 2

    sent = call(
        edges_kernel,
        shape((devices, 2 * half, res), BF16),
        (pair, gain_in[None], w_proj),
        scratch
        + [pltpu.VMEM(pair.shape, BF16), pltpu.VMEM((1, width), F32)]
        + [pltpu.VMEM(w_proj.shape, BF16), pltpu.VMEM((devices, 2 * half, res), BF16)]
        + [pltpu.SemaphoreType.DMA((3 + PIECES,))],
        outside=3,
        leave=True,
        limit=62,
    )
    sent, pair, cotangent = hold(sent, pair, cotangent)
    got = exchange(sent)

    turned = shape((rows, width, res), BF16)
    normed, factor, grad_proj_out, scaled = call(
        prepare_kernel,
        (
            turned,
            shape((rows, 5 * width, res), F32),
            turned,
            shape((res // LANES, width * rows, LANES), F32),
        ),
        (pair, cotangent, gain_in[None], gain_out[None], w_proj, w_out),
        flops=2 * rows * res * width * 6 * width,
    )
    got, normed, factor, grad_proj_out, scaled = hold(got, normed, factor, grad_proj_out, scaled)
    edge = shape((share, devices * rows, res), BF16)
    sent, left, right = call(
        functools.partial(triangle_kernel, share, rows),
        (shape((devices, half, res), BF16), edge, edge),
        (got,),
    )
    triangle = exchange(sent)
    sent = call(
        functools.partial(norm_grad_kernel, rows),
        shape((devices, half, res), BF16),
        (triangle, scaled),
    )
    got = exchange(sent)
    sent = call(
        functools.partial(edge_grads_kernel, share, rows),
        shape((devices, 2 * half, res), BF16),
        (got, left, right),
    )
    got = exchange(sent)
    sent = call(
        weight_grads_kernel,
        shape((devices, 6 * width // devices, width), BF16),
        (got, factor, normed, triangle, cotangent, grad_proj_out, gain_out[None], w_out),
        scratch + scratch[:1],
    )
    sums = exchange(sent)
    mine = jnp.sum(sums.astype(F32), axis=0).astype(BF16)
    mine = jnp.broadcast_to(mine[None], (devices,) + mine.shape)
    mine, edge_grads, factor, triangle = hold(mine, got, factor, triangle)
    full = exchange(mine)
    grad_pair, update = call(
        pair_grad_kernel,
        [shape((rows, res, width), BF16)] * 2,
        (edge_grads, factor, pair, triangle, cotangent)
        + (gain_in[None], gain_out[None], w_proj, w_out),
        scratch + scratch[:1],
        flops=2 * rows * res * width * 6 * width,
    )
    grad_w_proj, grad_w_out, grad_gain_in, grad_gain_out = call(
        finish_kernel,
        (
            shape((width, 5 * width), F32),
            shape((width, width), F32),
            shape((1, width), F32),
            shape((1, width), F32),
        ),
        (full, w_proj, w_out, gain_in[None], gain_out[None]),
    )
    return (update, grad_pair, grad_gain_in[0], grad_w_proj, grad_gain_out[0], grad_w_out)


def solution(mesh):
    devices = mesh.shape["dap"]

    def program(*args):
        return local(devices, *args)

    in_specs = (P(("dp", "dap"), None, None), P(), P(), P(), P(), P(("dp", "dap"), None, None))
    out_specs = (
        P(("dp", "dap"), None, None),
        P(("dp", "dap"), None, None),
        P("dp"),
        P("dp", None),
        P("dp"),
        P("dp", None),
    )
    return jax.shard_map(program, mesh=mesh, in_specs=in_specs, out_specs=out_specs, check_vma=False)
```

```python
import functools

import jax
import jax.numpy as jnp
from jax import lax
from jax.experimental import pallas as pl
from jax.experimental.pallas import tpu as pltpu
from jax.sharding import PartitionSpec as P

F32, BF16 = jnp.float32, jnp.bfloat16
EPS = 1e-05
LANES = 128
PIECES = 4
NT = (((1,), (1,)), ((), ()))


def places(devices):
    if devices % 16:
        return list(range(devices))
    order = []
    for n, high in enumerate(range(0, devices, 16)):
        for core in (n % 2, 1 - n % 2):
            order += [high + 2 * z + core for z in (0, 3, 4, 7, 1, 2, 5, 6)]
    return order


def exchange(values):
    groups = [places(values.shape[0])]
    return lax.all_to_all(values, "dap", 0, 0, tiled=True, axis_index_groups=groups)


def exchange_chips(values):
    chips = range(values.shape[0])
    if values.shape[0] % 8 == 0:
        chips = [high + z for high in chips[::8] for z in (0, 3, 4, 7, 1, 2, 5, 6)]
    groups = [[2 * chip + core for chip in chips] for core in range(2)]
    return lax.all_to_all(values, "dap", 0, 0, tiled=True, axis_index_groups=groups)


def swap(values):
    devices = lax.axis_size("dap")
    return lax.ppermute(values, "dap", [(d, d ^ 1) for d in range(devices)])


def hold(*values):
    return lax.optimization_barrier(values)


def call(kernel, out_shape, operands, scratch=(), flops=0, outside=0, limit=16, scalars=0, leave=False):
    leaves = out_shape if isinstance(out_shape, (tuple, list)) else [out_shape]
    moved = sum(a.size * a.dtype.itemsize for a in list(operands) + list(leaves))
    spec = pl.BlockSpec(memory_space=pltpu.VMEM)
    if leave:
        out_specs = pl.BlockSpec(memory_space=pl.ANY)
    else:
        out_specs = [spec] * len(out_shape) if isinstance(out_shape, (tuple, list)) else spec
    return pl.pallas_call(
        kernel,
        out_shape=out_shape,
        in_specs=[pl.BlockSpec(memory_space=pltpu.HBM)] * outside
        + [pl.BlockSpec(memory_space=pltpu.SMEM)] * scalars
        + [spec] * (len(operands) - outside - scalars),
        out_specs=out_specs,
        scratch_shapes=list(scratch),
        cost_estimate=pl.CostEstimate(flops=flops, bytes_accessed=moved, transcendentals=0),
        compiler_params=pltpu.CompilerParams(vmem_limit_bytes=limit * 1024 * 1024),
    )(*operands)


def norm_rows(values):
    width = values.shape[0]
    shifted = values - jnp.sum(values, axis=0, keepdims=True) * (1.0 / width)
    variance = jnp.sum(shifted * shifted, axis=0, keepdims=True) * (1.0 / width)
    inv_std = lax.rsqrt(variance + EPS)
    return shifted * inv_std, inv_std


def put_row(ref, i, rows, values):
    for h in range(ref.shape[0]):
        spots = pl.ds(i, values.shape[0], stride=rows)
        ref[h, spots, :] = values[:, h * LANES : (h + 1) * LANES]


def take_row(ref, i, rows):
    spots = pl.ds(i, ref.shape[1] // rows, stride=rows)
    return jnp.concatenate([ref[h, spots, :] for h in range(ref.shape[0])], axis=1)


def fill(got_ref, left_ref, right_ref):
    devices, both, _ = got_ref.shape
    half = both // 2
    for n, ref in enumerate((left_ref, right_ref)):
        for h in range(ref.shape[0]):
            block = got_ref[:, n * half : (n + 1) * half, h * LANES : (h + 1) * LANES]
            ref[h] = block.astype(F32).reshape(devices * half, LANES)


def edges_kernel(
    pair_hbm, gain_hbm, weight_hbm, sent_hbm, left_ref, right_ref, pair_ref, gain_ref, weight_ref, sent_ref, sems
):
    rows, res, width = pair_ref.shape
    devices = sent_ref.shape[0]
    half = sent_ref.shape[1] // 2
    pairs = ((weight_hbm, weight_ref), (gain_hbm, gain_ref), (pair_hbm, pair_ref))
    copies = [
        pltpu.make_async_copy(source, target, sems.at[n])
        for n, (source, target) in enumerate(pairs)
    ]
    for copy in copies:
        copy.start()
    copies[0].wait()
    weight = weight_ref[:, : 4 * width].astype(F32).T.astype(BF16)
    copies[1].wait()
    gain = gain_ref[...].T
    copies[2].wait()
    for i in range(rows):
        centred, _ = norm_rows(pair_ref[i].T.astype(F32))
        normed = (centred * gain).astype(BF16)
        out = jnp.dot(weight, normed, preferred_element_type=F32)
        put_row(left_ref, i, rows, jax.nn.sigmoid(out[width : 2 * width]) * out[:width])
        put_row(right_ref, i, rows, jax.nn.sigmoid(out[3 * width :]) * out[2 * width : 3 * width])
    step = devices // PIECES
    copies = []
    for piece in range(PIECES):
        slots = pl.ds(piece * step, step)
        for n, ref in enumerate((left_ref, right_ref)):
            for h in range(res // LANES):
                block = ref[h, pl.ds(piece * step * half, step * half), :]
                block = block.reshape(step, half, LANES).astype(BF16)
                sent_ref[slots, n * half : (n + 1) * half, h * LANES : (h + 1) * LANES] = block
        copy = pltpu.make_async_copy(sent_ref.at[slots], sent_hbm.at[slots], sems.at[3 + piece])
        copy.start()
        copies.append(copy)
    for copy in copies:
        copy.wait()


def prepare_kernel(
    pair_ref,
    cot_ref,
    gain_in_ref,
    gain_out_ref,
    weight_ref,
    w_out_ref,
    normed_ref,
    factor_ref,
    grad_out_ref,
    scaled_ref,
):
    rows, res, width = pair_ref.shape
    weight = weight_ref[...].astype(F32).T.astype(BF16)
    w_out = w_out_ref[...]
    gain_in, gain_out = gain_in_ref[...].T, gain_out_ref[...].T
    for i in range(rows):
        centred, _ = norm_rows(pair_ref[i].astype(F32).T)
        normed = (centred * gain_in).astype(BF16)
        normed_ref[i] = normed
        out = jnp.dot(weight, normed, preferred_element_type=F32)
        for side in range(2):
            first = 2 * side * width
            sig = jax.nn.sigmoid(out[first + width : first + 2 * width])
            factor_ref[i, first : first + width, :] = sig
            factor_ref[i, first + width : first + 2 * width, :] = (
                out[first : first + width] * sig * (1.0 - sig)
            )
        gate = jax.nn.sigmoid(out[4 * width :])
        factor_ref[i, 4 * width :, :] = gate
        grad_out = (cot_ref[i].astype(F32).T * gate).astype(BF16)
        grad_out_ref[i] = grad_out
        scaled = jnp.dot(w_out, grad_out, preferred_element_type=F32) * gain_out
        scaled = scaled - jnp.sum(scaled, axis=0, keepdims=True) * (1.0 / width)
        put_row(scaled_ref, i, rows, scaled)


def reorder(block, order):
    return jnp.stack([block[m] for m in order], axis=0)


def matrices_of(ref, first, share, rows, in_order=False):
    devices, _, res = ref.shape
    block = ref[:, first : first + share * rows, :].astype(F32)
    if in_order:
        order = places(devices)
        block = reorder(block, [order.index(d) for d in range(devices)])
    block = block.reshape(devices, share, rows, res)
    return [block[:, c].reshape(devices * rows, res).astype(BF16) for c in range(share)]


def store_matrices(ref, first, values, rows, in_order=False):
    devices, _, res = ref.shape
    block = jnp.stack([v.reshape(devices, rows, res) for v in values], axis=1)
    if in_order:
        block = reorder(block, places(devices))
    ref[:, first : first + len(values) * rows, :] = block.reshape(
        devices, len(values) * rows, res
    ).astype(BF16)


def triangle_kernel(share, rows, got_ref, sent_ref, left_ref, right_ref):
    half = share * rows
    left = matrices_of(got_ref, 0, share, rows)
    right = matrices_of(got_ref, half, share, rows, in_order=True)
    for c in range(share):
        left_ref[c] = left[c]
        right_ref[c] = right[c]
    out = [lax.dot_general(a, b, NT, preferred_element_type=F32) for a, b in zip(left, right)]
    store_matrices(sent_ref, 0, out, rows)


def norm_grad_kernel(rows, got_ref, scaled_ref, sent_ref):
    devices, block, res = got_ref.shape
    share = block // rows
    width = devices * share

    def over_share(values):
        return jnp.sum(values.reshape(share, rows, res), axis=0)

    zero = jnp.zeros((rows, res), F32)

    def scaled_of(d):
        spots = pl.ds(pl.multiple_of(d * block, block), block)
        return jnp.concatenate([scaled_ref[h, spots, :] for h in range(res // LANES)], axis=1)

    def add_up(d, carry):
        return carry + over_share(got_ref[d].astype(F32))

    mean = lax.fori_loop(0, devices, add_up, zero, unroll=4) * (1.0 / width)
    mean = jnp.concatenate([mean] * share, axis=0)

    def second(d, carry):
        shifted = got_ref[d].astype(F32) - mean
        return (
            carry[0] + over_share(shifted * shifted),
            carry[1] + over_share(shifted * scaled_of(d)),
        )

    variance, product = lax.fori_loop(0, devices, second, (zero, zero), unroll=4)
    inv_std = lax.rsqrt(variance * (1.0 / width) + EPS)
    product = product * (1.0 / width) * inv_std * inv_std * inv_std
    inv_std = jnp.concatenate([inv_std] * share, axis=0)
    product = jnp.concatenate([product] * share, axis=0)

    def write(d, carry):
        shifted = got_ref[d].astype(F32) - mean
        sent_ref[d] = (inv_std * scaled_of(d) - shifted * product).astype(BF16)
        return carry

    lax.fori_loop(0, devices, write, 0, unroll=4)


def edge_grads_kernel(share, rows, got_ref, left_ref, right_ref, sent_ref):
    grads = matrices_of(got_ref, 0, share, rows)
    left_grads, right_grads = [], []
    for c in range(share):
        left_grads.append(jnp.dot(grads[c], right_ref[c], preferred_element_type=F32))
        turned = grads[c].astype(F32).T.astype(BF16)
        right_grads.append(jnp.dot(turned, left_ref[c], preferred_element_type=F32))
    store_matrices(sent_ref, 0, left_grads, rows)
    store_matrices(sent_ref, share * rows, right_grads, rows, in_order=True)


def turn(triangle_ref, turned_ref):
    devices, half, _ = triangle_ref.shape
    for h in range(turned_ref.shape[0]):
        block = triangle_ref[:, :, h * LANES : (h + 1) * LANES]
        turned_ref[h] = block.astype(F32).reshape(devices * half, LANES)


def gate_grads(i, rows, factor_ref, cot_ref, gain_out, w_out, turned_ref):
    width = w_out.shape[0]
    centred, _ = norm_rows(take_row(turned_ref, i, rows))
    out_normed = (centred * gain_out).astype(BF16)
    gate = factor_ref[i, 4 * width :, :]
    update = gate * jnp.dot(w_out, out_normed, preferred_element_type=F32)
    grad_gate = (cot_ref[i].astype(F32).T * update * (1.0 - gate)).astype(BF16)
    return out_normed, update, grad_gate


def edge_parts(i, rows, factor_ref, left_ref, right_ref):
    left, right = take_row(left_ref, i, rows), take_row(right_ref, i, rows)
    width = left.shape[0]
    return [
        (grad * factor_ref[i, b * width : (b + 1) * width, :]).astype(BF16)
        for b, grad in enumerate((left, left, right, right))
    ]


def weight_grads_kernel(
    core_ref,
    got_ref,
    factor_ref,
    normed_ref,
    triangle_ref,
    cot_ref,
    grad_out_ref,
    gain_out_ref,
    w_out_ref,
    keep_ref,
    send_ref,
    left_ref,
    right_ref,
    turned_ref,
    halves_ref,
):
    rows = normed_ref.shape[0]
    fill(got_ref, left_ref, right_ref)
    turn(triangle_ref, turned_ref)
    w_out = w_out_ref[...].astype(F32).T.astype(BF16)
    gain_out = gain_out_ref[...].T
    total = None
    for i in range(rows):
        out_normed, _, grad_gate = gate_grads(
            i, rows, factor_ref, cot_ref, gain_out, w_out, turned_ref
        )
        grads = edge_parts(i, rows, factor_ref, left_ref, right_ref) + [grad_gate]
        pairs = [(normed_ref[i], grad) for grad in grads] + [(out_normed, grad_out_ref[i])]
        parts = [lax.dot_general(x, y, NT, preferred_element_type=F32) for x, y in pairs]
        total = parts if total is None else [x + y for x, y in zip(total, parts)]
    halves_ref[0] = jnp.concatenate(total[:3], axis=0)
    halves_ref[1] = jnp.concatenate(total[3:], axis=0)
    core = core_ref[0]
    keep_ref[...] = halves_ref[core]
    send_ref[...] = halves_ref[1 - core].astype(BF16)


def add_kernel(keep_ref, other_ref, sent_ref):
    total = keep_ref[...] + other_ref[...].astype(F32)
    sent_ref[...] = total.astype(BF16).reshape(sent_ref.shape)


def pair_grad_kernel(
    got_ref,
    factor_ref,
    pair_ref,
    triangle_ref,
    cot_ref,
    gain_in_ref,
    gain_out_ref,
    weight_ref,
    w_out_ref,
    out_ref,
    update_ref,
    left_ref,
    right_ref,
    turned_ref,
):
    rows, _, width = pair_ref.shape
    fill(got_ref, left_ref, right_ref)
    turn(triangle_ref, turned_ref)
    weight = weight_ref[...]
    w_out = w_out_ref[...].astype(F32).T.astype(BF16)
    gain_in, gain_out = gain_in_ref[...].T, gain_out_ref[...].T
    for i in range(rows):
        _, update, grad_gate = gate_grads(
            i, rows, factor_ref, cot_ref, gain_out, w_out, turned_ref
        )
        update_ref[i] = update.T.astype(BF16)
        grads = edge_parts(i, rows, factor_ref, left_ref, right_ref) + [grad_gate]
        grads = jnp.concatenate(grads, axis=0)
        scaled = jnp.dot(weight, grads, preferred_element_type=F32) * gain_in
        centred, inv_std = norm_rows(pair_ref[i].astype(F32).T)
        first = jnp.sum(scaled, axis=0, keepdims=True) * (1.0 / width)
        second = jnp.sum(scaled * centred, axis=0, keepdims=True) * (1.0 / width)
        grad_pair = inv_std * (scaled - first - centred * second)
        out_ref[i] = grad_pair.T.astype(BF16)


def sum_kernel(got_ref, sent_ref):
    total = got_ref[0].astype(F32)
    for m in range(1, got_ref.shape[0]):
        total = total + got_ref[m].astype(F32)
    total = total.astype(BF16)
    for m in range(sent_ref.shape[0]):
        sent_ref[m] = total


def finish_kernel(
    core_ref, own_ref, other_ref, weight_ref, w_out_ref, gain_in_ref, gain_out_ref, *outs
):
    grad_weight_ref, grad_out_ref, grad_gain_in_ref, grad_gain_out_ref, halves_ref = outs
    width = w_out_ref.shape[0]
    core = core_ref[0]
    halves_ref[core] = own_ref[...].astype(F32).reshape(3 * width, width)
    halves_ref[1 - core] = other_ref[...].astype(F32).reshape(3 * width, width)
    full = halves_ref[...].reshape(6 * width, width)
    weight = weight_ref[...].astype(F32)
    total = jnp.zeros((width, width), F32)
    for b in range(5):
        block = full[b * width : (b + 1) * width]
        grad_weight_ref[:, b * width : (b + 1) * width] = block
        total = total + block * weight[:, b * width : (b + 1) * width]
    block = full[5 * width :]
    grad_out_ref[...] = block
    total_out = block * w_out_ref[...].astype(F32)
    grad_gain_in_ref[...] = jnp.sum(total.T, axis=0, keepdims=True) / gain_in_ref[...]
    grad_gain_out_ref[...] = jnp.sum(total_out.T, axis=0, keepdims=True) / gain_out_ref[...]


def local(devices, pair, gain_in, w_proj, gain_out, w_out, cotangent):
    width = gain_out.shape[0]
    rows, res, _ = pair.shape
    share = width // devices
    half = share * rows
    shape = jax.ShapeDtypeStruct
    scratch = [pltpu.VMEM((res // LANES, width * rows, LANES), F32)] * 2

    sent = call(
        edges_kernel,
        shape((devices, 2 * half, res), BF16),
        (pair, gain_in[None], w_proj),
        scratch
        + [pltpu.VMEM(pair.shape, BF16), pltpu.VMEM((1, width), F32)]
        + [pltpu.VMEM(w_proj.shape, BF16), pltpu.VMEM((devices, 2 * half, res), BF16)]
        + [pltpu.SemaphoreType.DMA((3 + PIECES,))],
        outside=3,
        leave=True,
        limit=62,
    )
    core = lax.rem(lax.axis_index("dap"), 2).astype(jnp.int32)[None]
    sent, pair, cotangent, core = hold(sent, pair, cotangent, core)
    got = exchange(sent)

    turned = shape((rows, width, res), BF16)
    normed, factor, grad_proj_out, scaled = call(
        prepare_kernel,
        (
            turned,
            shape((rows, 5 * width, res), F32),
            turned,
            shape((res // LANES, width * rows, LANES), F32),
        ),
        (pair, cotangent, gain_in[None], gain_out[None], w_proj, w_out),
        flops=2 * rows * res * width * 6 * width,
    )
    got, normed, factor, grad_proj_out, scaled, core = hold(
        got, normed, factor, grad_proj_out, scaled, core
    )
    edge = shape((share, devices * rows, res), BF16)
    sent, left, right = call(
        functools.partial(triangle_kernel, share, rows),
        (shape((devices, half, res), BF16), edge, edge),
        (got,),
    )
    triangle = exchange(sent)
    sent = call(
        functools.partial(norm_grad_kernel, rows),
        shape((devices, half, res), BF16),
        (triangle, scaled),
    )
    got = exchange(sent)
    sent = call(
        functools.partial(edge_grads_kernel, share, rows),
        shape((devices, 2 * half, res), BF16),
        (got, left, right),
    )
    got = exchange(sent)
    chips = devices // 2
    half_shape = (3 * width, width)
    keep, send = call(
        weight_grads_kernel,
        (shape(half_shape, F32), shape(half_shape, BF16)),
        (core, got, factor, normed, triangle, cotangent, grad_proj_out, gain_out[None], w_out),
        scratch + scratch[:1] + [pltpu.VMEM((2,) + half_shape, F32)],
        scalars=1,
    )
    sent = call(add_kernel, shape((chips, 3 * width // chips, width), BF16), (keep, swap(send)))
    sums = exchange_chips(sent)
    mine = call(sum_kernel, shape(sums.shape, BF16), (sums,))
    mine, edge_grads, factor, triangle = hold(mine, got, factor, triangle)
    own = exchange_chips(mine)
    grad_pair, update = call(
        pair_grad_kernel,
        [shape((rows, res, width), BF16)] * 2,
        (edge_grads, factor, pair, triangle, cotangent)
        + (gain_in[None], gain_out[None], w_proj, w_out),
        scratch + scratch[:1],
        flops=2 * rows * res * width * 6 * width,
    )
    own, grad_pair, update = hold(own, grad_pair, update)
    grad_w_proj, grad_w_out, grad_gain_in, grad_gain_out = call(
        finish_kernel,
        (
            shape((width, 5 * width), F32),
            shape((width, width), F32),
            shape((1, width), F32),
            shape((1, width), F32),
        ),
        (core, own, swap(own), w_proj, w_out, gain_in[None], gain_out[None]),
        [pltpu.VMEM((2,) + half_shape, F32)],
        scalars=1,
    )
    return (update, grad_pair, grad_gain_in[0], grad_w_proj, grad_gain_out[0], grad_w_out)


def solution(mesh):
    devices = mesh.shape["dap"]

    def program(*args):
        return local(devices, *args)

    in_specs = (P(("dp", "dap"), None, None), P(), P(), P(), P(), P(("dp", "dap"), None, None))
    out_specs = (
        P(("dp", "dap"), None, None),
        P(("dp", "dap"), None, None),
        P("dp"),
        P("dp", None),
        P("dp"),
        P("dp", None),
    )
    return jax.shard_map(program, mesh=mesh, in_specs=in_specs, out_specs=out_specs, check_vma=False)
```

```python
import functools

import jax
import jax.numpy as jnp
from jax import lax
from jax.experimental import pallas as pl
from jax.experimental.pallas import tpu as pltpu
from jax.sharding import PartitionSpec as P

F32, BF16 = jnp.float32, jnp.bfloat16
EPS = 1e-05
LANES = 128
PIECES = 4
NT = (((1,), (1,)), ((), ()))


def places(devices):
    if devices % 16:
        return list(range(devices))
    order = []
    for n, high in enumerate(range(0, devices, 16)):
        for core in (n % 2, 1 - n % 2):
            order += [high + 2 * z + core for z in (0, 3, 4, 7, 1, 2, 5, 6)]
    return order


def exchange(values):
    groups = [places(values.shape[0])]
    return lax.all_to_all(values, "dap", 0, 0, tiled=True, axis_index_groups=groups)


def chips_of(members):
    chips = range(members)
    if members % 8 == 0:
        chips = [high + z for high in chips[::8] for z in (0, 3, 4, 7, 1, 2, 5, 6)]
    return list(chips)


def exchange_chips(values):
    chips = chips_of(values.shape[0])
    groups = [[2 * chip + core for chip in chips] for core in range(2)]
    return lax.all_to_all(values, "dap", 0, 0, tiled=True, axis_index_groups=groups)


def swap(values):
    devices = lax.axis_size("dap")
    return lax.ppermute(values, "dap", [(d, d ^ 1) for d in range(devices)])


def hold(*values):
    return lax.optimization_barrier(values)


def call(kernel, out_shape, operands, scratch=(), flops=0, outside=0, limit=16, scalars=0, leave=False):
    leaves = out_shape if isinstance(out_shape, (tuple, list)) else [out_shape]
    moved = sum(a.size * a.dtype.itemsize for a in list(operands) + list(leaves))
    spec = pl.BlockSpec(memory_space=pltpu.VMEM)
    if leave:
        out_specs = pl.BlockSpec(memory_space=pl.ANY)
    else:
        out_specs = [spec] * len(out_shape) if isinstance(out_shape, (tuple, list)) else spec
    return pl.pallas_call(
        kernel,
        out_shape=out_shape,
        in_specs=[pl.BlockSpec(memory_space=pltpu.HBM)] * outside
        + [pl.BlockSpec(memory_space=pltpu.SMEM)] * scalars
        + [spec] * (len(operands) - outside - scalars),
        out_specs=out_specs,
        scratch_shapes=list(scratch),
        cost_estimate=pl.CostEstimate(flops=flops, bytes_accessed=moved, transcendentals=0),
        compiler_params=pltpu.CompilerParams(vmem_limit_bytes=limit * 1024 * 1024),
    )(*operands)


def norm_rows(values):
    width = values.shape[0]
    shifted = values - jnp.sum(values, axis=0, keepdims=True) * (1.0 / width)
    variance = jnp.sum(shifted * shifted, axis=0, keepdims=True) * (1.0 / width)
    inv_std = lax.rsqrt(variance + EPS)
    return shifted * inv_std, inv_std


def put_row(ref, i, rows, values):
    for h in range(ref.shape[0]):
        spots = pl.ds(i, values.shape[0], stride=rows)
        ref[h, spots, :] = values[:, h * LANES : (h + 1) * LANES]


def take_row(ref, i, rows):
    spots = pl.ds(i, ref.shape[1] // rows, stride=rows)
    return jnp.concatenate([ref[h, spots, :] for h in range(ref.shape[0])], axis=1)


def fill(got_ref, left_ref, right_ref):
    devices, both, _ = got_ref.shape
    half = both // 2
    for n, ref in enumerate((left_ref, right_ref)):
        for h in range(ref.shape[0]):
            block = got_ref[:, n * half : (n + 1) * half, h * LANES : (h + 1) * LANES]
            ref[h] = block.astype(F32).reshape(devices * half, LANES)


def edges_kernel(
    pair_hbm, gain_hbm, weight_hbm, sent_hbm, left_ref, right_ref, pair_ref, gain_ref, weight_ref, sent_ref, sems
):
    rows, res, width = pair_ref.shape
    devices = sent_ref.shape[0]
    half = sent_ref.shape[1] // 2
    pairs = ((weight_hbm, weight_ref), (gain_hbm, gain_ref), (pair_hbm, pair_ref))
    copies = [
        pltpu.make_async_copy(source, target, sems.at[n])
        for n, (source, target) in enumerate(pairs)
    ]
    for copy in copies:
        copy.start()
    copies[0].wait()
    weight = weight_ref[:, : 4 * width].astype(F32).T.astype(BF16)
    copies[1].wait()
    gain = gain_ref[...].T
    copies[2].wait()
    for i in range(rows):
        centred, _ = norm_rows(pair_ref[i].T.astype(F32))
        normed = (centred * gain).astype(BF16)
        out = jnp.dot(weight, normed, preferred_element_type=F32)
        put_row(left_ref, i, rows, jax.nn.sigmoid(out[width : 2 * width]) * out[:width])
        put_row(right_ref, i, rows, jax.nn.sigmoid(out[3 * width :]) * out[2 * width : 3 * width])
    step = devices // PIECES
    copies = []
    for piece in range(PIECES):
        slots = pl.ds(piece * step, step)
        for n, ref in enumerate((left_ref, right_ref)):
            for h in range(res // LANES):
                block = ref[h, pl.ds(piece * step * half, step * half), :]
                block = block.reshape(step, half, LANES).astype(BF16)
                sent_ref[slots, n * half : (n + 1) * half, h * LANES : (h + 1) * LANES] = block
        copy = pltpu.make_async_copy(sent_ref.at[slots], sent_hbm.at[slots], sems.at[3 + piece])
        copy.start()
        copies.append(copy)
    for copy in copies:
        copy.wait()


def prepare_kernel(
    pair_ref,
    cot_ref,
    gain_in_ref,
    gain_out_ref,
    weight_ref,
    w_out_ref,
    normed_ref,
    factor_ref,
    grad_out_ref,
    scaled_ref,
):
    rows, res, width = pair_ref.shape
    weight = weight_ref[...].astype(F32).T.astype(BF16)
    w_out = w_out_ref[...]
    gain_in, gain_out = gain_in_ref[...].T, gain_out_ref[...].T
    for i in range(rows):
        centred, _ = norm_rows(pair_ref[i].astype(F32).T)
        normed = (centred * gain_in).astype(BF16)
        normed_ref[i] = normed
        out = jnp.dot(weight, normed, preferred_element_type=F32)
        for side in range(2):
            first = 2 * side * width
            sig = jax.nn.sigmoid(out[first + width : first + 2 * width])
            factor_ref[i, first : first + width, :] = sig
            factor_ref[i, first + width : first + 2 * width, :] = (
                out[first : first + width] * sig * (1.0 - sig)
            )
        gate = jax.nn.sigmoid(out[4 * width :])
        factor_ref[i, 4 * width :, :] = gate
        grad_out = (cot_ref[i].astype(F32).T * gate).astype(BF16)
        grad_out_ref[i] = grad_out
        scaled = jnp.dot(w_out, grad_out, preferred_element_type=F32) * gain_out
        scaled = scaled - jnp.sum(scaled, axis=0, keepdims=True) * (1.0 / width)
        put_row(scaled_ref, i, rows, scaled)


def reorder(block, order):
    return jnp.stack([block[m] for m in order], axis=0)


def matrices_of(ref, first, share, rows, in_order=False):
    devices, _, res = ref.shape
    block = ref[:, first : first + share * rows, :].astype(F32)
    if in_order:
        order = places(devices)
        block = reorder(block, [order.index(d) for d in range(devices)])
    block = block.reshape(devices, share, rows, res)
    return [block[:, c].reshape(devices * rows, res).astype(BF16) for c in range(share)]


def store_matrices(ref, first, values, rows, in_order=False):
    devices, _, res = ref.shape
    block = jnp.stack([v.reshape(devices, rows, res) for v in values], axis=1)
    if in_order:
        block = reorder(block, places(devices))
    ref[:, first : first + len(values) * rows, :] = block.reshape(
        devices, len(values) * rows, res
    ).astype(BF16)


def triangle_kernel(share, rows, got_ref, sent_ref, left_ref, right_ref):
    half = share * rows
    left = matrices_of(got_ref, 0, share, rows)
    right = matrices_of(got_ref, half, share, rows, in_order=True)
    for c in range(share):
        left_ref[c] = left[c]
        right_ref[c] = right[c]
    out = [lax.dot_general(a, b, NT, preferred_element_type=F32) for a, b in zip(left, right)]
    store_matrices(sent_ref, 0, out, rows)


def norm_grad_kernel(rows, got_ref, scaled_ref, sent_ref):
    devices, block, res = got_ref.shape
    share = block // rows
    width = devices * share

    def over_share(values):
        return jnp.sum(values.reshape(share, rows, res), axis=0)

    zero = jnp.zeros((rows, res), F32)

    def scaled_of(d):
        spots = pl.ds(pl.multiple_of(d * block, block), block)
        return jnp.concatenate([scaled_ref[h, spots, :] for h in range(res // LANES)], axis=1)

    def add_up(d, carry):
        return carry + over_share(got_ref[d].astype(F32))

    mean = lax.fori_loop(0, devices, add_up, zero, unroll=4) * (1.0 / width)
    mean = jnp.concatenate([mean] * share, axis=0)

    def second(d, carry):
        shifted = got_ref[d].astype(F32) - mean
        return (
            carry[0] + over_share(shifted * shifted),
            carry[1] + over_share(shifted * scaled_of(d)),
        )

    variance, product = lax.fori_loop(0, devices, second, (zero, zero), unroll=4)
    inv_std = lax.rsqrt(variance * (1.0 / width) + EPS)
    product = product * (1.0 / width) * inv_std * inv_std * inv_std
    inv_std = jnp.concatenate([inv_std] * share, axis=0)
    product = jnp.concatenate([product] * share, axis=0)

    def write(d, carry):
        shifted = got_ref[d].astype(F32) - mean
        sent_ref[d] = (inv_std * scaled_of(d) - shifted * product).astype(BF16)
        return carry

    lax.fori_loop(0, devices, write, 0, unroll=4)


def edge_grads_kernel(share, rows, got_ref, left_ref, right_ref, sent_ref):
    grads = matrices_of(got_ref, 0, share, rows)
    left_grads, right_grads = [], []
    for c in range(share):
        left_grads.append(jnp.dot(grads[c], right_ref[c], preferred_element_type=F32))
        turned = grads[c].astype(F32).T.astype(BF16)
        right_grads.append(jnp.dot(turned, left_ref[c], preferred_element_type=F32))
    store_matrices(sent_ref, 0, left_grads, rows)
    store_matrices(sent_ref, share * rows, right_grads, rows, in_order=True)


def turn(triangle_ref, turned_ref):
    devices, half, _ = triangle_ref.shape
    for h in range(turned_ref.shape[0]):
        block = triangle_ref[:, :, h * LANES : (h + 1) * LANES]
        turned_ref[h] = block.astype(F32).reshape(devices * half, LANES)


def gate_grads(i, rows, factor_ref, cot_ref, gain_out, w_out, turned_ref):
    width = w_out.shape[0]
    centred, _ = norm_rows(take_row(turned_ref, i, rows))
    out_normed = (centred * gain_out).astype(BF16)
    gate = factor_ref[i, 4 * width :, :]
    update = gate * jnp.dot(w_out, out_normed, preferred_element_type=F32)
    grad_gate = (cot_ref[i].astype(F32).T * update * (1.0 - gate)).astype(BF16)
    return out_normed, update, grad_gate


def edge_parts(i, rows, factor_ref, left_ref, right_ref):
    left, right = take_row(left_ref, i, rows), take_row(right_ref, i, rows)
    width = left.shape[0]
    return [
        (grad * factor_ref[i, b * width : (b + 1) * width, :]).astype(BF16)
        for b, grad in enumerate((left, left, right, right))
    ]


def weight_grads_kernel(
    core_ref,
    got_ref,
    factor_ref,
    normed_ref,
    triangle_ref,
    cot_ref,
    grad_out_ref,
    gain_out_ref,
    w_out_ref,
    keep_ref,
    send_ref,
    left_ref,
    right_ref,
    turned_ref,
    halves_ref,
):
    rows = normed_ref.shape[0]
    fill(got_ref, left_ref, right_ref)
    turn(triangle_ref, turned_ref)
    w_out = w_out_ref[...].astype(F32).T.astype(BF16)
    gain_out = gain_out_ref[...].T
    total = None
    for i in range(rows):
        out_normed, _, grad_gate = gate_grads(
            i, rows, factor_ref, cot_ref, gain_out, w_out, turned_ref
        )
        grads = edge_parts(i, rows, factor_ref, left_ref, right_ref) + [grad_gate]
        pairs = [(normed_ref[i], grad) for grad in grads] + [(out_normed, grad_out_ref[i])]
        parts = [lax.dot_general(x, y, NT, preferred_element_type=F32) for x, y in pairs]
        total = parts if total is None else [x + y for x, y in zip(total, parts)]
    halves_ref[0] = jnp.concatenate(total[:3], axis=0)
    halves_ref[1] = jnp.concatenate(total[3:], axis=0)
    core = core_ref[0]
    keep_ref[...] = halves_ref[core]
    send_ref[...] = halves_ref[1 - core].astype(BF16)


def add_kernel(keep_ref, other_ref, sent_ref):
    total = keep_ref[...] + other_ref[...].astype(F32)
    sent_ref[...] = total.astype(BF16).reshape(sent_ref.shape)


def pair_grad_kernel(
    got_ref,
    factor_ref,
    pair_ref,
    triangle_ref,
    cot_ref,
    gain_in_ref,
    gain_out_ref,
    weight_ref,
    w_out_ref,
    out_ref,
    update_ref,
    left_ref,
    right_ref,
    turned_ref,
):
    rows, _, width = pair_ref.shape
    fill(got_ref, left_ref, right_ref)
    turn(triangle_ref, turned_ref)
    weight = weight_ref[...]
    w_out = w_out_ref[...].astype(F32).T.astype(BF16)
    gain_in, gain_out = gain_in_ref[...].T, gain_out_ref[...].T
    for i in range(rows):
        _, update, grad_gate = gate_grads(
            i, rows, factor_ref, cot_ref, gain_out, w_out, turned_ref
        )
        update_ref[i] = update.T.astype(BF16)
        grads = edge_parts(i, rows, factor_ref, left_ref, right_ref) + [grad_gate]
        grads = jnp.concatenate(grads, axis=0)
        scaled = jnp.dot(weight, grads, preferred_element_type=F32) * gain_in
        centred, inv_std = norm_rows(pair_ref[i].astype(F32).T)
        first = jnp.sum(scaled, axis=0, keepdims=True) * (1.0 / width)
        second = jnp.sum(scaled * centred, axis=0, keepdims=True) * (1.0 / width)
        grad_pair = inv_std * (scaled - first - centred * second)
        out_ref[i] = grad_pair.T.astype(BF16)


def sum_kernel(got_ref, sent_ref):
    total = got_ref[0].astype(F32)
    for m in range(1, got_ref.shape[0]):
        total = total + got_ref[m].astype(F32)
    total = total.astype(BF16)
    for m in range(sent_ref.shape[0]):
        sent_ref[m] = total


def finish_kernel(
    full_ref, weight_ref, w_out_ref, gain_in_ref, gain_out_ref, *outs
):
    grad_weight_ref, grad_out_ref, grad_gain_in_ref, grad_gain_out_ref = outs
    width = w_out_ref.shape[0]
    devices = full_ref.shape[0]
    order = places(devices)
    slots = [order.index(2 * c + core) for core in range(2) for c in chips_of(devices // 2)]
    full = jnp.concatenate([full_ref[m].astype(F32) for m in slots], axis=0)
    weight = weight_ref[...].astype(F32)
    total = jnp.zeros((width, width), F32)
    for b in range(5):
        block = full[b * width : (b + 1) * width]
        grad_weight_ref[:, b * width : (b + 1) * width] = block
        total = total + block * weight[:, b * width : (b + 1) * width]
    block = full[5 * width :]
    grad_out_ref[...] = block
    total_out = block * w_out_ref[...].astype(F32)
    grad_gain_in_ref[...] = jnp.sum(total.T, axis=0, keepdims=True) / gain_in_ref[...]
    grad_gain_out_ref[...] = jnp.sum(total_out.T, axis=0, keepdims=True) / gain_out_ref[...]


def local(devices, pair, gain_in, w_proj, gain_out, w_out, cotangent):
    width = gain_out.shape[0]
    rows, res, _ = pair.shape
    share = width // devices
    half = share * rows
    shape = jax.ShapeDtypeStruct
    scratch = [pltpu.VMEM((res // LANES, width * rows, LANES), F32)] * 2

    sent = call(
        edges_kernel,
        shape((devices, 2 * half, res), BF16),
        (pair, gain_in[None], w_proj),
        scratch
        + [pltpu.VMEM(pair.shape, BF16), pltpu.VMEM((1, width), F32)]
        + [pltpu.VMEM(w_proj.shape, BF16), pltpu.VMEM((devices, 2 * half, res), BF16)]
        + [pltpu.SemaphoreType.DMA((3 + PIECES,))],
        outside=3,
        leave=True,
        limit=62,
    )
    core = lax.rem(lax.axis_index("dap"), 2).astype(jnp.int32)[None]
    sent, pair, cotangent, core = hold(sent, pair, cotangent, core)
    got = exchange(sent)

    turned = shape((rows, width, res), BF16)
    normed, factor, grad_proj_out, scaled = call(
        prepare_kernel,
        (
            turned,
            shape((rows, 5 * width, res), F32),
            turned,
            shape((res // LANES, width * rows, LANES), F32),
        ),
        (pair, cotangent, gain_in[None], gain_out[None], w_proj, w_out),
        flops=2 * rows * res * width * 6 * width,
    )
    got, normed, factor, grad_proj_out, scaled, core = hold(
        got, normed, factor, grad_proj_out, scaled, core
    )
    edge = shape((share, devices * rows, res), BF16)
    sent, left, right = call(
        functools.partial(triangle_kernel, share, rows),
        (shape((devices, half, res), BF16), edge, edge),
        (got,),
    )
    triangle = exchange(sent)
    sent = call(
        functools.partial(norm_grad_kernel, rows),
        shape((devices, half, res), BF16),
        (triangle, scaled),
    )
    got = exchange(sent)
    sent = call(
        functools.partial(edge_grads_kernel, share, rows),
        shape((devices, 2 * half, res), BF16),
        (got, left, right),
    )
    got = exchange(sent)
    chips = devices // 2
    half_shape = (3 * width, width)
    keep, send = call(
        weight_grads_kernel,
        (shape(half_shape, F32), shape(half_shape, BF16)),
        (core, got, factor, normed, triangle, cotangent, grad_proj_out, gain_out[None], w_out),
        scratch + scratch[:1] + [pltpu.VMEM((2,) + half_shape, F32)],
        scalars=1,
    )
    sent = call(add_kernel, shape((chips, 3 * width // chips, width), BF16), (keep, swap(send)))
    sums = exchange_chips(sent)
    mine = call(sum_kernel, shape((devices,) + sums.shape[1:], BF16), (sums,))
    mine, edge_grads, factor, triangle = hold(mine, got, factor, triangle)
    own = exchange(mine)
    grad_pair, update = call(
        pair_grad_kernel,
        [shape((rows, res, width), BF16)] * 2,
        (edge_grads, factor, pair, triangle, cotangent)
        + (gain_in[None], gain_out[None], w_proj, w_out),
        scratch + scratch[:1],
        flops=2 * rows * res * width * 6 * width,
    )
    own, grad_pair, update = hold(own, grad_pair, update)
    grad_w_proj, grad_w_out, grad_gain_in, grad_gain_out = call(
        finish_kernel,
        (
            shape((width, 5 * width), F32),
            shape((width, width), F32),
            shape((1, width), F32),
            shape((1, width), F32),
        ),
        (own, w_proj, w_out, gain_in[None], gain_out[None]),
    )
    return (update, grad_pair, grad_gain_in[0], grad_w_proj, grad_gain_out[0], grad_w_out)


def solution(mesh):
    devices = mesh.shape["dap"]

    def program(*args):
        return local(devices, *args)

    in_specs = (P(("dp", "dap"), None, None), P(), P(), P(), P(), P(("dp", "dap"), None, None))
    out_specs = (
        P(("dp", "dap"), None, None),
        P(("dp", "dap"), None, None),
        P("dp"),
        P("dp", None),
        P("dp"),
        P("dp", None),
    )
    return jax.shard_map(program, mesh=mesh, in_specs=in_specs, out_specs=out_specs, check_vma=False)
```
